32 devices in a mesh: dp: 16 (over z, y, core), tile: 2 (over x).
Axes of the slice: x: 2, y: 2, z: 4, core: 2. Of those that a mesh axis runs over, the one named last changes fastest.
Arguments:
- fields: bfloat16 [16, 48, 16, 1024], P('dp', 'tile'), may hold values from -6 to 6
- weights: bfloat16 [64, 16, 3, 3], replicated, may hold values from -0.5 to 0.5
- bias: float32 [64], replicated, may hold values from -1 to 1
- cotangent: bfloat16 [16, 48, 64, 1024], P('dp', 'tile'), may hold values from -6 to 6
- neighbours: int32 [48, 8], replicated, may hold values from 0 to 47
- rotations: int32 [48, 8], replicated, may hold values from 0 to 3
- tile_map: int32 [48], replicated, may hold values from 0 to 47, each once
Outputs:
- outputs: bfloat16 [16, 48, 64, 1024], P('dp', 'tile')
- grad_fields: bfloat16 [16, 48, 16, 1024], P('dp', 'tile')
- grad_weights: float32 [64, 16, 3, 3], replicated
- grad_bias: float32 [64], replicated
The draws below stay inside these ranges and needn't reach their ends.
Inputs may be any that keep to these rules, and one draw needn't show every extreme that they name: neighbours[t, k] is the tile across edge k of tile t (above, below, left, right) for k < 4, and at corner k - 4 (above left, above right, below left, below right) otherwise. `rotations`: counterclockwise quarter turns of the neighbour's tile as seen from tile t. Slot s of the tiled arrays holds tile tile_map[s]; every tile once; device i of tile holds slots i * 24 to (i + 1) * 24 - 1.
All inputs are finite; a program needn't handle non-finite values.
Results may differ from the reference program's by a relative error of at most 0.002.
Values may be sent and summed in bfloat16 or wider, within the bound.
A program may use at most 128 MiB of HBM per device.

```python
import math
import jax
import jax.numpy as jnp
from jax import lax

C_IN = 16
C_OUT = 64
TS = 32
TILES = 48
BATCH = 16


def touch_ends(array, key, least, largest):
    longest = array.shape.index(max(array.shape))
    spots = []
    for shift in (0, 1):
        where = [jax.random.randint(jax.random.fold_in(key, axis), (), 0, length) for axis, length in enumerate(array.shape)]
        where[longest] = (where[longest] + shift) % array.shape[longest]
        spots.append(tuple(where))
    return array.at[spots[0]].set(least).at[spots[1]].set(largest)


def levels(rng, dims, pieces, low, largest):
    gain, own = 1.0, jax.random.fold_in(rng, 6)
    for dim, parts in pieces:
        draws = jnp.exp(jax.random.uniform(jax.random.fold_in(own, dim), (parts,), jnp.float32, low / len(pieces), largest / len(pieces)))
        gain = gain * jnp.repeat(draws, dims[dim] // parts).reshape([-1 if axis == dim else 1 for axis in range(len(dims))])
    return gain


def scatter_about(key, dims, deviation, most, cuts=(), held_as=jnp.bfloat16):
    gain = levels(key, dims, cuts, -0.22, 0.18) if cuts else 1.0
    array = jax.random.normal(key, dims, jnp.float32) * deviation * gain
    return jnp.minimum(jnp.maximum(array, -most), most).astype(held_as)


def setup_inputs(seed: int = 0) -> dict:
    seeds = jax.random.split(jax.random.key(seed), 8)
    fields = scatter_about(seeds[0], (BATCH, TILES, C_IN, TS * TS), 1.0, 6.0, ((0, 16), (1, 2)))
    weights = scatter_about(seeds[1], (C_OUT, C_IN, 3, 3), (C_IN * 9) ** -0.5, 0.5)
    bias = jnp.clip(jax.random.uniform(seeds[2], (C_OUT,), jnp.float32, -1.0, 1.0), -1.0, 1.0)
    cotangent = scatter_about(seeds[3], (BATCH, TILES, C_OUT, TS * TS), 1.0, 6.0, ((0, 16), (1, 2)))
    neighbours = touch_ends(jax.random.randint(seeds[4], (TILES, 8), 0, TILES), jax.random.fold_in(seeds[4], 1), 0, TILES - 1).astype(jnp.int32)
    rotations = touch_ends(jax.random.randint(seeds[5], (TILES, 8), 0, 4), jax.random.fold_in(seeds[5], 1), 0, 3).astype(jnp.int32)
    tile_map = jax.random.permutation(seeds[6], TILES).astype(jnp.int32)
    return {"fields": fields, "weights": weights, "bias": bias, "cotangent": cotangent, "neighbours": neighbours, "rotations": rotations, "tile_map": tile_map}


def build_padded(sample, slot_nbr, slot_rot):
    turned = jnp.stack([jnp.rot90(sample, quarter, axes=(-2, -1)) for quarter in range(4)])
    strips = jnp.stack([turned[..., -1, :], turned[..., 0, :], turned[..., :, -1], turned[..., :, 0]], axis=2)
    corners = jnp.stack([turned[..., -1, -1], turned[..., -1, 0], turned[..., 0, -1], turned[..., 0, 0]], axis=2)
    sides = [strips[slot_rot[:, k], slot_nbr[:, k], k] for k in range(4)]
    tips = [corners[slot_rot[:, k], slot_nbr[:, k], k - 4] for k in range(4, 8)]
    top_row = jnp.concatenate([tips[0][..., None], sides[0], tips[1][..., None]], axis=-1)
    low_row = jnp.concatenate([tips[2][..., None], sides[1], tips[3][..., None]], axis=-1)
    middle = jnp.concatenate([sides[2][..., None], sample, sides[3][..., None]], axis=-1)
    return jnp.concatenate([top_row[..., None, :], middle, low_row[..., None, :]], axis=-2)

def reference(fields, weights, bias, cotangent, neighbours, rotations, tile_map):
    fields = fields.reshape(BATCH, TILES, C_IN, TS, TS)
    cotangent = cotangent.reshape(BATCH, TILES, C_OUT, TS, TS)
    places = jnp.arange(TILES, dtype=jnp.int32)
    inverse = lax.optimization_barrier(jnp.sum(jnp.where(tile_map[None, :] == places[:, None], places[None, :], 0), axis=1)).astype(jnp.int32)
    slot_nbr = inverse[neighbours[tile_map]].astype(jnp.int32)
    slot_rot = rotations[tile_map].astype(jnp.int32)
    kernel = weights.astype(jnp.float32)
    factor = 1.0 / math.sqrt(BATCH * TILES * TS * TS)

    def forward(sample, kern, shift):
        padded = build_padded(sample, slot_nbr, slot_rot)
        response = lax.conv_general_dilated(padded, kern, (1, 1), 'VALID', dimension_numbers=('NCHW', 'OIHW', 'NCHW'), precision=lax.Precision.HIGHEST)
        return response + shift[None, :, None, None]

    def one_sample(carry, items):
        sample, cot_sample = items
        pre, pullback = jax.vjp(forward, sample.astype(jnp.float32), kernel, bias)
        grad_in, grad_kern, grad_shift = pullback(cot_sample.astype(jnp.float32))
        return ((carry[0] + grad_kern, carry[1] + grad_shift), (pre.astype(jnp.bfloat16), grad_in.astype(jnp.bfloat16)))
    start = (jnp.zeros((C_OUT, C_IN, 3, 3), jnp.float32), jnp.zeros((C_OUT,), jnp.float32))
    sums, stacked = lax.scan(one_sample, start, (fields, cotangent))
    outputs = stacked[0].reshape(BATCH, TILES, C_OUT, TS * TS)
    grad_fields = stacked[1].reshape(BATCH, TILES, C_IN, TS * TS)
    return (outputs, grad_fields, sums[0] * factor, sums[1] * factor)
```

```python
import math

import jax
import jax.numpy as jnp
import numpy as np
from jax import lax
from jax.experimental import pallas as pl
from jax.experimental.pallas import tpu as pltpu
from jax.sharding import PartitionSpec as P

TS = 32


edge_table = np.array(
    [
        [1, 2, 0, 3],
        [0, 3, 1, 2],
        [3, 1, 2, 0],
        [2, 0, 3, 1],
        [1, 1, 0, 0],
        [1, 0, 0, 1],
        [0, 1, 1, 0],
        [0, 0, 1, 1],
    ],
    dtype=np.int32,
)
flip_table = np.array(
    [
        [0, 0, 1, 1],
        [0, 0, 1, 1],
        [0, 1, 1, 0],
        [0, 1, 1, 0],
        [1, 0, 0, 1],
        [0, 0, 1, 1],
        [1, 1, 0, 0],
        [0, 1, 1, 0],
    ],
    dtype=np.int32,
)


def slot_tables(tile_map, neighbours, rotations):
    total_slots = tile_map.shape[0]
    places = jnp.arange(total_slots, dtype=jnp.int32)
    onehot = (tile_map[:, None] == places[None, :]).astype(jnp.int32)
    inverse = jnp.sum(
        (tile_map[None, :] == places[:, None]).astype(jnp.int32) * places[None, :], axis=1
    )
    tile_nbr = jnp.sum(onehot[:, :, None] * neighbours[None], axis=1)
    tile_rot = jnp.sum(onehot[:, :, None] * rotations[None], axis=1)
    slot_nbr = jnp.sum(
        (tile_nbr[:, :, None] == places[None, None, :]).astype(jnp.int32) * inverse[None, None, :],
        axis=2,
    )
    matches = (tile_rot[:, :, None] == jnp.arange(4, dtype=jnp.int32)).astype(jnp.int32)
    edge_code = jnp.sum(matches * jnp.asarray(edge_table)[None], axis=-1)
    flip_code = jnp.sum(matches * jnp.asarray(flip_table)[None], axis=-1)
    return (slot_nbr, edge_code, flip_code)


CELLS = TS * TS
LANES = 128
VMEM_LIMIT = 50 * 1024 * 1024


def column_picker():
    m = np.zeros((CELLS, LANES), np.float32)
    for h in range(TS):
        m[h * TS, 2 * TS + h] = 1
        m[h * TS + TS - 1, 3 * TS + h] = 1
    return m


def strip_variants():
    m = np.zeros((LANES, 8 * LANES), np.float32)
    for edge in range(4):
        for flip in range(2):
            for rep in range(4):
                for t in range(TS):
                    at = TS - 1 - t if flip else t
                    m[edge * TS + at, (edge * 2 + flip) * LANES + rep * TS + t] = 1
    return m


def rim_images():
    m = np.zeros((2 * LANES, CELLS + 3 * LANES), np.float32)
    for h in range(TS):
        m[2 * TS + h, h * TS] = 1
        m[3 * TS + h, h * TS + TS - 1] = 1
    tops = [LANES] + list(range(TS)) + [LANES + TS]
    lows = [LANES + 2 * TS] + list(range(TS, 2 * TS)) + [LANES + 3 * TS]
    for col_tap in range(3):
        for w in range(TS):
            m[tops[w + col_tap], CELLS + col_tap * LANES + w] = 1
            m[lows[w + col_tap], CELLS + col_tap * LANES + 3 * TS + w] = 1
    return m


def edge_images():
    m = np.zeros((LANES, CELLS), np.float32)
    for t in range(TS):
        m[t, t] = 1
        m[TS + t, (TS - 1) * TS + t] = 1
        m[2 * TS + t, t * TS] = 1
        m[3 * TS + t, t * TS + TS - 1] = 1
    return np.concatenate([m, m], axis=0)


def const(m):
    return jnp.asarray(m.astype(jnp.bfloat16))


def dot(a, b):
    return jnp.dot(a, b, preferred_element_type=jnp.float32)


def lane_ids(width):
    return lax.broadcasted_iota(jnp.int32, (16, width), 1)


def edges_kernel(x_ref, pick_ref, q_ref):
    n = x_ref.shape[0]
    x = x_ref[...].reshape(n * 16, CELLS)
    cols = dot(x, pick_ref[...])
    first = x[:, :LANES].astype(jnp.float32)
    last = pltpu.roll(x[:, CELLS - LANES :].astype(jnp.float32), 2 * TS, 1)
    lane = lax.broadcasted_iota(jnp.int32, (n * 16, LANES), 1)
    q = jnp.where(lane < TS, first, jnp.where(lane < 2 * TS, last, cols))
    q_ref[...] = q.astype(jnp.bfloat16).reshape(n, 16, LANES)


def back_kernel(g_ref, wt_ref, pick_ref, inner_ref, p_ref):
    lane = lane_ids(CELLS)
    w = lane % TS
    blk = lane_ids(LANES)
    for t in range(g_ref.shape[0]):
        z = dot(wt_ref[...], g_ref[t])
        rows, rim = [], []
        for a in range(3):
            z0, z1, z2 = (z[(a * 3 + c) * 16 : (a * 3 + c + 1) * 16] for c in range(3))
            rows.append(
                z1
                + jnp.where(w != TS - 1, pltpu.roll(z0, CELLS - 1, 1), 0.0)
                + jnp.where(w != 0, pltpu.roll(z2, 1, 1), 0.0)
            )
            rim.append(jnp.where(w == 0, z0, jnp.where(w == TS - 1, z2, 0.0)))

        def rows_added(y):
            up = jnp.where(lane < CELLS - TS, pltpu.roll(y[0], CELLS - TS, 1), 0.0)
            down = jnp.where(lane >= TS, pltpu.roll(y[2], TS, 1), 0.0)
            return y[1] + up + down

        inner_ref[t] = rows_added(rows)
        cols = dot(rows_added(rim).astype(jnp.bfloat16), pick_ref[...])
        first = rows[0][:, :LANES]
        last = pltpu.roll(rows[2][:, CELLS - LANES :], 2 * TS, 1)
        edge = jnp.where(blk < TS, first, jnp.where(blk < 2 * TS, last, cols))
        c0 = rim[0][:, :LANES]
        c2 = rim[2][:, CELLS - LANES :]
        corner = jnp.where(blk == 0, c0, 0.0)
        corner += jnp.where(blk == TS, pltpu.roll(c0, 1, 1), 0.0)
        corner += jnp.where(blk == 2 * TS, pltpu.roll(c2, LANES - TS, 1), 0.0)
        corner += jnp.where(blk == 3 * TS, pltpu.roll(c2, LANES - TS + 1, 1), 0.0)
        p_ref[t, :, :LANES] = edge.astype(jnp.bfloat16)
        p_ref[t, :, LANES:] = corner.astype(jnp.bfloat16)


def front_kernel(
    slots, fsrc_ref, q_ref, var_ref, img_ref, x_ref, g_ref, w_ref, bias_ref,
    out_ref, dw_ref, v_ref, rim_ref, ri_ref, col_ref,
):
    step = pl.program_id(0)
    blk = lane_ids(LANES)

    @pl.when(step == 0)
    def _():
        total = q_ref.shape[0]
        q = q_ref[...].reshape(total * 16, LANES)
        for j in range(8):
            got = dot(q, var_ref[:, j * LANES : (j + 1) * LANES])
            v_ref[j * total : (j + 1) * total] = got.reshape(total, 16, LANES)
        for s in range(slots):
            for half in range(2):
                parts = [v_ref[fsrc_ref[s * 8 + half * 4 + k]] for k in range(4)]
                rim = jnp.where(
                    blk < 2 * TS,
                    jnp.where(blk < TS, parts[0], parts[1]),
                    jnp.where(blk < 3 * TS, parts[2], parts[3]),
                )
                rim_ref[s, :, half * LANES : (half + 1) * LANES] = rim.astype(jnp.bfloat16)
        ri = dot(rim_ref[...].reshape(slots * 16, 2 * LANES), img_ref[...])
        ri_ref[...] = ri.reshape(slots, 16, CELLS + 3 * LANES)
        dw_ref[...] = jnp.zeros_like(dw_ref)
        for t in range(col_ref.shape[0]):
            col_ref[t, 144:160, :] = jnp.ones((16, CELLS), jnp.bfloat16)

    w = lane_ids(CELLS) % TS
    tiles = x_ref.shape[0]
    total = jnp.zeros(dw_ref.shape, jnp.float32)
    for t in range(tiles):
        s = step * tiles + t
        x = x_ref[t].astype(jnp.float32)
        lr = ri_ref[s, :, :CELLS]
        mids = [
            jnp.where(w == 0, lr, pltpu.roll(x, 1, 1)),
            x,
            jnp.where(w == TS - 1, lr, pltpu.roll(x, CELLS - 1, 1)),
        ]
        for c in range(3):
            rim = ri_ref[s, :, CELLS + c * LANES : CELLS + (c + 1) * LANES]
            down = pltpu.roll(mids[c], TS, 1)
            up = pltpu.roll(mids[c], CELLS - TS, 1)
            down = jnp.concatenate(
                [jnp.where(blk < TS, rim, down[:, :LANES]), down[:, LANES:]], axis=1
            )
            up = jnp.concatenate(
                [up[:, : CELLS - LANES], jnp.where(blk >= 3 * TS, rim, up[:, CELLS - LANES :])],
                axis=1,
            )
            for a, tap in enumerate((down, mids[c], up)):
                row = (a * 3 + c) * 16
                col_ref[t, row : row + 16, :] = tap.astype(jnp.bfloat16)
        col = col_ref[t]
        out_ref[t] = (dot(w_ref[...], col[:144]) + bias_ref[...]).astype(jnp.bfloat16)
        total += lax.dot_general(
            g_ref[t], col, (((1,), (1,)), ((), ())), preferred_element_type=jnp.float32
        )
    dw_ref[...] += total


def finish_kernel(slots, bsrc_ref, bdst_ref, p_ref, var_ref, img_ref, inner_ref, out_ref, u_ref, acc_ref, r_ref):
    total = p_ref.shape[0]
    blk = lane_ids(LANES)
    for kind in range(2):
        p = p_ref[:, :, kind * LANES : (kind + 1) * LANES].reshape(total * 16, LANES)
        for j in range(8):
            got = dot(p, var_ref[:, j * LANES : (j + 1) * LANES])
            at = (kind * 8 + j) * total
            u_ref[at : at + total] = got.reshape(total, 16, LANES)
    acc_ref[...] = jnp.zeros_like(acc_ref)

    def add(q, carry):
        for k in range(8):
            d = bdst_ref[q * 8 + k]
            acc_ref[d] = acc_ref[d] + u_ref[bsrc_ref[q * 8 + k]]
        return carry

    lax.fori_loop(0, total, add, 0)
    for s in range(slots):
        parts = [acc_ref[s * 4 + k] for k in range(4)]
        r = jnp.where(
            blk < 2 * TS,
            jnp.where(blk < TS, parts[0], parts[1]),
            jnp.where(blk < 3 * TS, parts[2], parts[3]),
        )
        hi = r.astype(jnp.bfloat16)
        r_ref[s, :, :LANES] = hi
        r_ref[s, :, LANES:] = (r - hi.astype(jnp.float32)).astype(jnp.bfloat16)
    add_in = dot(r_ref[...].reshape(slots * 16, 2 * LANES), img_ref[...])
    out = inner_ref[...].reshape(slots * 16, CELLS) + add_in
    out_ref[...] = out.astype(jnp.bfloat16).reshape(slots, 16, CELLS)


def params():
    return pltpu.CompilerParams(vmem_limit_bytes=VMEM_LIMIT)


def cost(flops, bytes_accessed):
    return pl.CostEstimate(flops=flops, bytes_accessed=bytes_accessed, transcendentals=0)


def body(fields, weights, bias, cotangent, neighbours, rotations, tile_map):
    batch_loc, slots, in_chans, cells = fields.shape
    out_chans = weights.shape[0]
    x = fields.reshape(slots, in_chans, cells)
    g = cotangent.reshape(slots, out_chans, cells)
    tiles = 3
    steps = slots // tiles
    f32, bf16 = jnp.float32, jnp.bfloat16
    pick = const(column_picker())
    variants = const(strip_variants())
    vmem = pl.BlockSpec(memory_space=pltpu.VMEM)
    smem = pl.BlockSpec(memory_space=pltpu.SMEM)

    def whole(*dims):
        return pl.BlockSpec(dims, lambda i, *_: (0,) * len(dims))

    def block(*dims):
        return pl.BlockSpec((tiles, *dims), lambda i, *_: (i,) + (0,) * len(dims))

    edges = pl.pallas_call(
        edges_kernel,
        out_shape=jax.ShapeDtypeStruct((slots, in_chans, LANES), bf16),
        in_specs=[vmem, vmem],
        out_specs=vmem,
        compiler_params=params(),
        cost_estimate=cost(slots * 16 * CELLS * 256, slots * 16 * CELLS * 2),
        name="edges",
    )(x, pick)
    all_edges = lax.all_gather(edges, "tile", axis=0, tiled=True)
    total = all_edges.shape[0]

    wt = weights.transpose(2, 3, 1, 0).reshape(9 * in_chans, out_chans)
    inner, rim_cot = pl.pallas_call(
        back_kernel,
        grid=(steps,),
        out_shape=(
            jax.ShapeDtypeStruct((slots, in_chans, cells), f32),
            jax.ShapeDtypeStruct((slots, in_chans, 2 * LANES), bf16),
        ),
        in_specs=[block(out_chans, cells), whole(*wt.shape), whole(*pick.shape)],
        out_specs=(block(in_chans, cells), block(in_chans, 2 * LANES)),
        compiler_params=params(),
        cost_estimate=cost(slots * 1024 * 144 * 128 * 8, slots * 64 * CELLS * 4),
        name="back",
    )(g, wt, pick)
    all_rims = lax.all_gather(rim_cot, "tile", axis=0, tiled=True)

    slot_nbr, edge_code, flip_code = slot_tables(tile_map, neighbours, rotations)
    base = lax.axis_index("tile") * slots
    src = (edge_code * 2 + flip_code) * total + slot_nbr
    fsrc = lax.dynamic_slice_in_dim(src, base, slots, 0).reshape(-1)
    here = slot_nbr - base
    bdst = jnp.where((here >= 0) & (here < slots), here * 4 + edge_code, slots * 4).reshape(-1)
    ks = jnp.arange(8, dtype=jnp.int32)[None, :]
    bsrc = ((ks * 2 + flip_code) * total + jnp.arange(total, dtype=jnp.int32)[:, None]).reshape(-1)

    wf = weights.transpose(0, 2, 3, 1).reshape(out_chans, 9 * in_chans)
    images = const(rim_images())
    outputs, sums = pl.pallas_call(
        lambda *refs: front_kernel(slots, *refs),
        grid_spec=pltpu.PrefetchScalarGridSpec(
            num_scalar_prefetch=1,
            grid=(steps,),
            in_specs=[
                whole(*all_edges.shape),
                whole(*variants.shape),
                whole(*images.shape),
                block(in_chans, cells),
                block(out_chans, cells),
                whole(*wf.shape),
                whole(out_chans, 1),
            ],
            out_specs=(block(out_chans, cells), whole(out_chans, 160)),
            scratch_shapes=[
                pltpu.VMEM((8 * total, in_chans, LANES), f32),
                pltpu.VMEM((slots, in_chans, 2 * LANES), bf16),
                pltpu.VMEM((slots, in_chans, CELLS + 3 * LANES), f32),
                pltpu.VMEM((tiles, 160, CELLS), bf16),
            ],
        ),
        out_shape=(
            jax.ShapeDtypeStruct((slots, out_chans, cells), bf16),
            jax.ShapeDtypeStruct((out_chans, 160), f32),
        ),
        compiler_params=params(),
        cost_estimate=cost(slots * 1024 * 144 * 256 * 8, slots * 64 * CELLS * 4),
        name="front",
    )(fsrc, all_edges, variants, images, x, g, wf, bias[:, None])
    factor = 1.0 / math.sqrt(
        batch_loc * lax.axis_size("dp") * slots * lax.axis_size("tile") * cells
    )
    sums = lax.psum(sums, ("dp", "tile")) * factor
    grad_weights = sums[:, :144].reshape(out_chans, 3, 3, in_chans).transpose(0, 3, 1, 2)
    grad_bias = sums[:, 144]

    edge_img = const(edge_images())
    grad_fields = pl.pallas_call(
        lambda *refs: finish_kernel(slots, *refs),
        out_shape=jax.ShapeDtypeStruct((slots, in_chans, cells), bf16),
        in_specs=[smem, smem, vmem, vmem, vmem, vmem],
        out_specs=vmem,
        scratch_shapes=[
            pltpu.VMEM((16 * total, in_chans, LANES), f32),
            pltpu.VMEM((4 * slots + 8, in_chans, LANES), f32),
            pltpu.VMEM((slots, in_chans, 2 * LANES), bf16),
        ],
        compiler_params=params(),
        cost_estimate=cost(slots * 1024 * 144 * 128 * 8, slots * 64 * CELLS * 4),
        name="finish",
    )(bsrc, bdst, all_rims, variants, edge_img, inner)
    return (
        outputs.reshape(cotangent.shape),
        grad_fields.reshape(fields.shape),
        grad_weights,
        grad_bias,
    )


def solution(mesh):
    placed = (P("dp", "tile", None, None), P(), P(), P("dp", "tile", None, None), P(), P(), P())
    return jax.shard_map(
        body,
        mesh=mesh,
        in_specs=placed,
        out_specs=(P("dp", "tile", None, None), P("dp", "tile", None, None), P(), P()),
        check_vma=False,
    )
```

```python
import math

import jax
import jax.numpy as jnp
import numpy as np
from jax import lax
from jax.experimental import pallas as pl
from jax.experimental.pallas import tpu as pltpu
from jax.sharding import PartitionSpec as P

TS = 32


edge_table = np.array(
    [
        [1, 2, 0, 3],
        [0, 3, 1, 2],
        [3, 1, 2, 0],
        [2, 0, 3, 1],
        [1, 1, 0, 0],
        [1, 0, 0, 1],
        [0, 1, 1, 0],
        [0, 0, 1, 1],
    ],
    dtype=np.int32,
)
flip_table = np.array(
    [
        [0, 0, 1, 1],
        [0, 0, 1, 1],
        [0, 1, 1, 0],
        [0, 1, 1, 0],
        [1, 0, 0, 1],
        [0, 0, 1, 1],
        [1, 1, 0, 0],
        [0, 1, 1, 0],
    ],
    dtype=np.int32,
)


def slot_tables(tile_map, neighbours, rotations):
    total_slots = tile_map.shape[0]
    places = jnp.arange(total_slots, dtype=jnp.int32)
    onehot = (tile_map[:, None] == places[None, :]).astype(jnp.int32)
    inverse = jnp.sum(
        (tile_map[None, :] == places[:, None]).astype(jnp.int32) * places[None, :], axis=1
    )
    tile_nbr = jnp.sum(onehot[:, :, None] * neighbours[None], axis=1)
    tile_rot = jnp.sum(onehot[:, :, None] * rotations[None], axis=1)
    slot_nbr = jnp.sum(
        (tile_nbr[:, :, None] == places[None, None, :]).astype(jnp.int32) * inverse[None, None, :],
        axis=2,
    )
    matches = (tile_rot[:, :, None] == jnp.arange(4, dtype=jnp.int32)).astype(jnp.int32)
    edge_code = jnp.sum(matches * jnp.asarray(edge_table)[None], axis=-1)
    flip_code = jnp.sum(matches * jnp.asarray(flip_table)[None], axis=-1)
    return (slot_nbr, edge_code, flip_code)


CELLS = TS * TS
LANES = 128
VMEM_LIMIT = 50 * 1024 * 1024


def column_picker():
    m = np.zeros((CELLS, LANES), np.float32)
    for h in range(TS):
        m[h * TS, 2 * TS + h] = 1
        m[h * TS + TS - 1, 3 * TS + h] = 1
    return m


def strip_variants():
    m = np.zeros((LANES, 8 * LANES), np.float32)
    for edge in range(4):
        for flip in range(2):
            for rep in range(4):
                for t in range(TS):
                    at = TS - 1 - t if flip else t
                    m[edge * TS + at, (edge * 2 + flip) * LANES + rep * TS + t] = 1
    return m


def rim_images():
    m = np.zeros((2 * LANES, CELLS + 3 * LANES), np.float32)
    for h in range(TS):
        m[2 * TS + h, h * TS] = 1
        m[3 * TS + h, h * TS + TS - 1] = 1
    tops = [LANES] + list(range(TS)) + [LANES + TS]
    lows = [LANES + 2 * TS] + list(range(TS, 2 * TS)) + [LANES + 3 * TS]
    for col_tap in range(3):
        for w in range(TS):
            m[tops[w + col_tap], CELLS + col_tap * LANES + w] = 1
            m[lows[w + col_tap], CELLS + col_tap * LANES + 3 * TS + w] = 1
    return m


def edge_images():
    m = np.zeros((LANES, CELLS), np.float32)
    for t in range(TS):
        m[t, t] = 1
        m[TS + t, (TS - 1) * TS + t] = 1
        m[2 * TS + t, t * TS] = 1
        m[3 * TS + t, t * TS + TS - 1] = 1
    return np.concatenate([m, m], axis=0)


def const(m):
    return jnp.asarray(m.astype(jnp.bfloat16))


def dot(a, b):
    return jnp.dot(a, b, preferred_element_type=jnp.float32)


def lane_ids(width):
    return lax.broadcasted_iota(jnp.int32, (16, width), 1)


def edges_kernel(x_ref, pick_ref, q_ref):
    n = x_ref.shape[0]
    x = x_ref[...].reshape(n * 16, CELLS)
    cols = dot(x, pick_ref[...])
    first = x[:, :LANES].astype(jnp.float32)
    last = pltpu.roll(x[:, CELLS - LANES :].astype(jnp.float32), 2 * TS, 1)
    lane = lax.broadcasted_iota(jnp.int32, (n * 16, LANES), 1)
    q = jnp.where(lane < TS, first, jnp.where(lane < 2 * TS, last, cols))
    q_ref[...] = q.astype(jnp.bfloat16).reshape(n, 16, LANES)


def back_kernel(g_ref, wt_ref, pick_ref, inner_ref, p_ref):
    lane = lane_ids(CELLS)
    w = lane % TS
    blk = lane_ids(LANES)
    for t in range(g_ref.shape[0]):
        z = dot(wt_ref[...], g_ref[t])
        rows, rim = [], []
        for a in range(3):
            z0, z1, z2 = (z[(a * 3 + c) * 16 : (a * 3 + c + 1) * 16] for c in range(3))
            rows.append(
                z1
                + jnp.where(w != TS - 1, pltpu.roll(z0, CELLS - 1, 1), 0.0)
                + jnp.where(w != 0, pltpu.roll(z2, 1, 1), 0.0)
            )
            rim.append(jnp.where(w == 0, z0, jnp.where(w == TS - 1, z2, 0.0)))

        def rows_added(y):
            up = jnp.where(lane < CELLS - TS, pltpu.roll(y[0], CELLS - TS, 1), 0.0)
            down = jnp.where(lane >= TS, pltpu.roll(y[2], TS, 1), 0.0)
            return y[1] + up + down

        inner_ref[t] = rows_added(rows)
        cols = dot(rows_added(rim).astype(jnp.bfloat16), pick_ref[...])
        first = rows[0][:, :LANES]
        last = pltpu.roll(rows[2][:, CELLS - LANES :], 2 * TS, 1)
        edge = jnp.where(blk < TS, first, jnp.where(blk < 2 * TS, last, cols))
        c0 = rim[0][:, :LANES]
        c2 = rim[2][:, CELLS - LANES :]
        corner = jnp.where(blk == 0, c0, 0.0)
        corner += jnp.where(blk == TS, pltpu.roll(c0, 1, 1), 0.0)
        corner += jnp.where(blk == 2 * TS, pltpu.roll(c2, LANES - TS, 1), 0.0)
        corner += jnp.where(blk == 3 * TS, pltpu.roll(c2, LANES - TS + 1, 1), 0.0)
        p_ref[t, :, :LANES] = edge.astype(jnp.bfloat16)
        p_ref[t, :, LANES:] = corner.astype(jnp.bfloat16)


def front_kernel(
    slots, fsrc_ref, q_ref, var_ref, img_ref, x_ref, g_ref, w_ref, bias_ref,
    out_ref, dw_ref, v_ref, rim_ref, ri_ref, col_ref,
):
    step = pl.program_id(0)
    blk = lane_ids(LANES)

    @pl.when(step == 0)
    def _():
        total = q_ref.shape[0]
        q = q_ref[...].reshape(total * 16, LANES)
        for j in range(8):
            got = dot(q, var_ref[:, j * LANES : (j + 1) * LANES])
            v_ref[j * total : (j + 1) * total] = got.reshape(total, 16, LANES)
        for s in range(slots):
            for half in range(2):
                parts = [v_ref[fsrc_ref[s * 8 + half * 4 + k]] for k in range(4)]
                rim = jnp.where(
                    blk < 2 * TS,
                    jnp.where(blk < TS, parts[0], parts[1]),
                    jnp.where(blk < 3 * TS, parts[2], parts[3]),
                )
                rim_ref[s, :, half * LANES : (half + 1) * LANES] = rim.astype(jnp.bfloat16)
        ri = dot(rim_ref[...].reshape(slots * 16, 2 * LANES), img_ref[...])
        ri_ref[...] = ri.reshape(slots, 16, CELLS + 3 * LANES)
        dw_ref[...] = jnp.zeros_like(dw_ref)
        for t in range(col_ref.shape[0]):
            col_ref[t, 144:160, :] = jnp.ones((16, CELLS), jnp.bfloat16)

    w = lane_ids(CELLS) % TS
    tiles = x_ref.shape[0]
    total = jnp.zeros(dw_ref.shape, jnp.float32)
    for t in range(tiles):
        s = step * tiles + t
        x = x_ref[t].astype(jnp.float32)
        lr = ri_ref[s, :, :CELLS]
        mids = [
            jnp.where(w == 0, lr, pltpu.roll(x, 1, 1)),
            x,
            jnp.where(w == TS - 1, lr, pltpu.roll(x, CELLS - 1, 1)),
        ]
        for c in range(3):
            rim = ri_ref[s, :, CELLS + c * LANES : CELLS + (c + 1) * LANES]
            down = pltpu.roll(mids[c], TS, 1)
            up = pltpu.roll(mids[c], CELLS - TS, 1)
            down = jnp.concatenate(
                [jnp.where(blk < TS, rim, down[:, :LANES]), down[:, LANES:]], axis=1
            )
            up = jnp.concatenate(
                [up[:, : CELLS - LANES], jnp.where(blk >= 3 * TS, rim, up[:, CELLS - LANES :])],
                axis=1,
            )
            for a, tap in enumerate((down, mids[c], up)):
                row = (a * 3 + c) * 16
                col_ref[t, row : row + 16, :] = tap.astype(jnp.bfloat16)
        col = col_ref[t]
        out_ref[t] = (dot(w_ref[...], col[:144]) + bias_ref[...]).astype(jnp.bfloat16)
        total += lax.dot_general(
            g_ref[t], col, (((1,), (1,)), ((), ())), preferred_element_type=jnp.float32
        )
    dw_ref[...] += total


def finish_kernel(slots, bsrc_ref, bdst_ref, p_ref, var_ref, img_ref, inner_ref, out_ref, u_ref, acc_ref, r_ref):
    total = p_ref.shape[0]
    blk = lane_ids(LANES)
    for kind in range(2):
        p = p_ref[:, :, kind * LANES : (kind + 1) * LANES].reshape(total * 16, LANES)
        for j in range(8):
            got = dot(p, var_ref[:, j * LANES : (j + 1) * LANES])
            at = (kind * 8 + j) * total
            u_ref[at : at + total] = got.reshape(total, 16, LANES)
    acc_ref[...] = jnp.zeros_like(acc_ref)

    def add(q, carry):
        for k in range(8):
            d = bdst_ref[q * 8 + k]
            acc_ref[d] = acc_ref[d] + u_ref[bsrc_ref[q * 8 + k]]
        return carry

    lax.fori_loop(0, total, add, 0)
    for s in range(slots):
        parts = [acc_ref[s * 4 + k] for k in range(4)]
        r = jnp.where(
            blk < 2 * TS,
            jnp.where(blk < TS, parts[0], parts[1]),
            jnp.where(blk < 3 * TS, parts[2], parts[3]),
        )
        hi = r.astype(jnp.bfloat16)
        r_ref[s, :, :LANES] = hi
        r_ref[s, :, LANES:] = (r - hi.astype(jnp.float32)).astype(jnp.bfloat16)
    add_in = dot(r_ref[...].reshape(slots * 16, 2 * LANES), img_ref[...])
    out = inner_ref[...].reshape(slots * 16, CELLS) + add_in
    out_ref[...] = out.astype(jnp.bfloat16).reshape(slots, 16, CELLS)


def sum_kernel(dp_size, tile_size, factor, in_ref, out_ref, near_ref, far_ref, near_send, near_recv, far_send, far_recv):
    dp, tile = lax.axis_index("dp"), lax.axis_index("tile")
    pairs = dp_size // 2
    core, hi = lax.rem(dp, 2), dp // 2
    near_count = 2 * tile_size

    def near_peer(j):
        return (hi * 2 + lax.rem(core + j % 2, 2), lax.rem(tile + j // 2, tile_size))

    def far_peer(j):
        return (lax.rem(hi + j, pairs) * 2 + core, tile)

    peers = [near_peer(j) for j in range(1, near_count)] + [far_peer(j) for j in range(1, pairs)]
    barrier = pltpu.get_barrier_semaphore()
    for peer in peers:
        pl.semaphore_signal(barrier, inc=1, device_id=peer, device_id_type=pl.DeviceIdType.MESH)

    rows = in_ref.shape[0]
    quarter = rows // 4
    rest = in_ref[:, LANES:]
    packed = jnp.concatenate(
        [
            in_ref[:, :LANES],
            jnp.concatenate([rest[k * quarter : (k + 1) * quarter] for k in range(4)], axis=1),
        ],
        axis=0,
    )
    pl.semaphore_wait(barrier, len(peers))

    def exchange(value, ref, me, count, peer_of, send, recv):
        ref[me] = value
        copies = []
        for j in range(1, count):
            copy = pltpu.make_async_remote_copy(
                src_ref=ref.at[me],
                dst_ref=ref.at[me],
                send_sem=send.at[j],
                recv_sem=recv.at[j],
                device_id=peer_of(j),
                device_id_type=pl.DeviceIdType.MESH,
            )
            copy.start()
            copies.append(copy)
        for copy in copies:
            copy.wait_recv()
        total = ref[0]
        for j in range(1, count):
            total = total + ref[j]
        return total, copies

    near, near_copies = exchange(
        packed, near_ref, core * tile_size + tile, near_count, near_peer, near_send, near_recv
    )
    far, far_copies = exchange(near, far_ref, hi, pairs, far_peer, far_send, far_recv)
    far = far * factor
    out_ref[:, :LANES] = far[:rows]
    for k in range(4):
        out_ref[k * quarter : (k + 1) * quarter, LANES:] = far[rows:, k * 32 : (k + 1) * 32]
    for copy in near_copies + far_copies:
        copy.wait_send()


def params():
    return pltpu.CompilerParams(vmem_limit_bytes=VMEM_LIMIT)


def cost(flops, bytes_accessed):
    return pl.CostEstimate(flops=flops, bytes_accessed=bytes_accessed, transcendentals=0)


def body(fields, weights, bias, cotangent, neighbours, rotations, tile_map):
    batch_loc, slots, in_chans, cells = fields.shape
    out_chans = weights.shape[0]
    x = fields.reshape(slots, in_chans, cells)
    g = cotangent.reshape(slots, out_chans, cells)
    tiles = 3
    steps = slots // tiles
    f32, bf16 = jnp.float32, jnp.bfloat16
    pick = const(column_picker())
    variants = const(strip_variants())
    vmem = pl.BlockSpec(memory_space=pltpu.VMEM)
    smem = pl.BlockSpec(memory_space=pltpu.SMEM)

    def whole(*dims):
        return pl.BlockSpec(dims, lambda i, *_: (0,) * len(dims))

    def block(*dims):
        return pl.BlockSpec((tiles, *dims), lambda i, *_: (i,) + (0,) * len(dims))

    edges = pl.pallas_call(
        edges_kernel,
        out_shape=jax.ShapeDtypeStruct((slots, in_chans, LANES), bf16),
        in_specs=[vmem, vmem],
        out_specs=vmem,
        compiler_params=params(),
        cost_estimate=cost(slots * 16 * CELLS * 256, slots * 16 * CELLS * 2),
        name="edges",
    )(x, pick)
    all_edges = lax.all_gather(edges, "tile", axis=0, tiled=True)
    total = all_edges.shape[0]

    wt = weights.transpose(2, 3, 1, 0).reshape(9 * in_chans, out_chans)
    inner, rim_cot = pl.pallas_call(
        back_kernel,
        grid=(steps,),
        out_shape=(
            jax.ShapeDtypeStruct((slots, in_chans, cells), f32),
            jax.ShapeDtypeStruct((slots, in_chans, 2 * LANES), bf16),
        ),
        in_specs=[block(out_chans, cells), whole(*wt.shape), whole(*pick.shape)],
        out_specs=(block(in_chans, cells), block(in_chans, 2 * LANES)),
        compiler_params=params(),
        cost_estimate=cost(slots * 1024 * 144 * 128 * 8, slots * 64 * CELLS * 4),
        name="back",
    )(g, wt, pick)
    all_rims = lax.all_gather(rim_cot, "tile", axis=0, tiled=True)

    slot_nbr, edge_code, flip_code = slot_tables(tile_map, neighbours, rotations)
    base = lax.axis_index("tile") * slots
    src = (edge_code * 2 + flip_code) * total + slot_nbr
    fsrc = lax.dynamic_slice_in_dim(src, base, slots, 0).reshape(-1)
    here = slot_nbr - base
    bdst = jnp.where((here >= 0) & (here < slots), here * 4 + edge_code, slots * 4).reshape(-1)
    ks = jnp.arange(8, dtype=jnp.int32)[None, :]
    bsrc = ((ks * 2 + flip_code) * total + jnp.arange(total, dtype=jnp.int32)[:, None]).reshape(-1)

    wf = weights.transpose(0, 2, 3, 1).reshape(out_chans, 9 * in_chans)
    images = const(rim_images())
    outputs, sums = pl.pallas_call(
        lambda *refs: front_kernel(slots, *refs),
        grid_spec=pltpu.PrefetchScalarGridSpec(
            num_scalar_prefetch=1,
            grid=(steps,),
            in_specs=[
                whole(*all_edges.shape),
                whole(*variants.shape),
                whole(*images.shape),
                block(in_chans, cells),
                block(out_chans, cells),
                whole(*wf.shape),
                whole(out_chans, 1),
            ],
            out_specs=(block(out_chans, cells), whole(out_chans, 160)),
            scratch_shapes=[
                pltpu.VMEM((8 * total, in_chans, LANES), f32),
                pltpu.VMEM((slots, in_chans, 2 * LANES), bf16),
                pltpu.VMEM((slots, in_chans, CELLS + 3 * LANES), f32),
                pltpu.VMEM((tiles, 160, CELLS), bf16),
            ],
        ),
        out_shape=(
            jax.ShapeDtypeStruct((slots, out_chans, cells), bf16),
            jax.ShapeDtypeStruct((out_chans, 160), f32),
        ),
        compiler_params=params(),
        cost_estimate=cost(slots * 1024 * 144 * 256 * 8, slots * 64 * CELLS * 4),
        name="front",
    )(fsrc, all_edges, variants, images, x, g, wf, bias[:, None])
    factor = 1.0 / math.sqrt(
        batch_loc * lax.axis_size("dp") * slots * lax.axis_size("tile") * cells
    )
    dp_size, tile_size = lax.axis_size("dp"), lax.axis_size("tile")
    packed_rows = out_chans + out_chans // 4
    sums = pl.pallas_call(
        lambda *refs: sum_kernel(dp_size, tile_size, factor, *refs),
        out_shape=jax.ShapeDtypeStruct((out_chans, 160), f32),
        in_specs=[vmem],
        out_specs=vmem,
        scratch_shapes=[
            pltpu.VMEM((2 * tile_size, packed_rows, LANES), f32),
            pltpu.VMEM((dp_size // 2, packed_rows, LANES), f32),
            pltpu.SemaphoreType.DMA((2 * tile_size,)),
            pltpu.SemaphoreType.DMA((2 * tile_size,)),
            pltpu.SemaphoreType.DMA((dp_size // 2,)),
            pltpu.SemaphoreType.DMA((dp_size // 2,)),
        ],
        compiler_params=pltpu.CompilerParams(
            collective_id=0, has_side_effects=True, vmem_limit_bytes=VMEM_LIMIT
        ),
        name="sums",
    )(sums)
    grad_weights = sums[:, :144].reshape(out_chans, 3, 3, in_chans).transpose(0, 3, 1, 2)
    grad_bias = sums[:, 144]

    edge_img = const(edge_images())
    grad_fields = pl.pallas_call(
        lambda *refs: finish_kernel(slots, *refs),
        out_shape=jax.ShapeDtypeStruct((slots, in_chans, cells), bf16),
        in_specs=[smem, smem, vmem, vmem, vmem, vmem],
        out_specs=vmem,
        scratch_shapes=[
            pltpu.VMEM((16 * total, in_chans, LANES), f32),
            pltpu.VMEM((4 * slots + 8, in_chans, LANES), f32),
            pltpu.VMEM((slots, in_chans, 2 * LANES), bf16),
        ],
        compiler_params=params(),
        cost_estimate=cost(slots * 1024 * 144 * 128 * 8, slots * 64 * CELLS * 4),
        name="finish",
    )(bsrc, bdst, all_rims, variants, edge_img, inner)
    return (
        outputs.reshape(cotangent.shape),
        grad_fields.reshape(fields.shape),
        grad_weights,
        grad_bias,
    )


def solution(mesh):
    placed = (P("dp", "tile", None, None), P(), P(), P("dp", "tile", None, None), P(), P(), P())
    return jax.shard_map(
        body,
        mesh=mesh,
        in_specs=placed,
        out_specs=(P("dp", "tile", None, None), P("dp", "tile", None, None), P(), P()),
        check_vma=False,
    )
```

```python
import math

import jax
import jax.numpy as jnp
import numpy as np
from jax import lax
from jax.experimental import pallas as pl
from jax.experimental.pallas import tpu as pltpu
from jax.sharding import PartitionSpec as P

TS = 32


edge_table = np.array(
    [
        [1, 2, 0, 3],
        [0, 3, 1, 2],
        [3, 1, 2, 0],
        [2, 0, 3, 1],
        [1, 1, 0, 0],
        [1, 0, 0, 1],
        [0, 1, 1, 0],
        [0, 0, 1, 1],
    ],
    dtype=np.int32,
)
flip_table = np.array(
    [
        [0, 0, 1, 1],
        [0, 0, 1, 1],
        [0, 1, 1, 0],
        [0, 1, 1, 0],
        [1, 0, 0, 1],
        [0, 0, 1, 1],
        [1, 1, 0, 0],
        [0, 1, 1, 0],
    ],
    dtype=np.int32,
)


def slot_tables(tile_map, neighbours, rotations):
    total_slots = tile_map.shape[0]
    places = jnp.arange(total_slots, dtype=jnp.int32)
    onehot = (tile_map[:, None] == places[None, :]).astype(jnp.int32)
    inverse = jnp.sum(
        (tile_map[None, :] == places[:, None]).astype(jnp.int32) * places[None, :], axis=1
    )
    tile_nbr = jnp.sum(onehot[:, :, None] * neighbours[None], axis=1)
    tile_rot = jnp.sum(onehot[:, :, None] * rotations[None], axis=1)
    slot_nbr = jnp.sum(
        (tile_nbr[:, :, None] == places[None, None, :]).astype(jnp.int32) * inverse[None, None, :],
        axis=2,
    )
    matches = (tile_rot[:, :, None] == jnp.arange(4, dtype=jnp.int32)).astype(jnp.int32)
    edge_code = jnp.sum(matches * jnp.asarray(edge_table)[None], axis=-1)
    flip_code = jnp.sum(matches * jnp.asarray(flip_table)[None], axis=-1)
    return (slot_nbr, edge_code, flip_code)


CELLS = TS * TS
LANES = 128
VMEM_LIMIT = 50 * 1024 * 1024


def column_picker():
    m = np.zeros((CELLS, LANES), np.float32)
    for h in range(TS):
        m[h * TS, 2 * TS + h] = 1
        m[h * TS + TS - 1, 3 * TS + h] = 1
    return m


def strip_variants():
    m = np.zeros((LANES, 8 * LANES), np.float32)
    for edge in range(4):
        for flip in range(2):
            for rep in range(4):
                for t in range(TS):
                    at = TS - 1 - t if flip else t
                    m[edge * TS + at, (edge * 2 + flip) * LANES + rep * TS + t] = 1
    return m


def rim_images():
    m = np.zeros((2 * LANES, CELLS + 3 * LANES), np.float32)
    for h in range(TS):
        m[2 * TS + h, h * TS] = 1
        m[3 * TS + h, h * TS + TS - 1] = 1
    tops = [LANES] + list(range(TS)) + [LANES + TS]
    lows = [LANES + 2 * TS] + list(range(TS, 2 * TS)) + [LANES + 3 * TS]
    for col_tap in range(3):
        for w in range(TS):
            m[tops[w + col_tap], CELLS + col_tap * LANES + w] = 1
            m[lows[w + col_tap], CELLS + col_tap * LANES + 3 * TS + w] = 1
    return m


def edge_images():
    m = np.zeros((LANES, CELLS), np.float32)
    for t in range(TS):
        m[t, t] = 1
        m[TS + t, (TS - 1) * TS + t] = 1
        m[2 * TS + t, t * TS] = 1
        m[3 * TS + t, t * TS + TS - 1] = 1
    return np.concatenate([m, m], axis=0)


def const(m):
    return jnp.asarray(m.astype(jnp.bfloat16))


def dot(a, b):
    return jnp.dot(a, b, preferred_element_type=jnp.float32)


def lane_ids(width):
    return lax.broadcasted_iota(jnp.int32, (16, width), 1)


def gather_kernel(
    tile_size, x_ref, g_ref, wt_ref, pick_ref, inner_ref, edges_ref, rims_ref,
    q_all, p_all, q_send, q_recv, p_send, p_recv,
):
    step = pl.program_id(0)
    slots, tiles = x_ref.shape[0], g_ref.shape[0]
    steps = slots // tiles
    dp, tile = lax.axis_index("dp"), lax.axis_index("tile")
    base = tile * slots
    barrier = pltpu.get_barrier_semaphore()
    mesh_ids = pl.DeviceIdType.MESH

    def peer(j):
        return (dp, lax.rem(tile + j, tile_size))

    def edges_copy(j):
        part = q_all.at[pl.ds(base, slots)]
        return pltpu.make_async_remote_copy(
            src_ref=part, dst_ref=part, send_sem=q_send.at[j], recv_sem=q_recv.at[j],
            device_id=peer(j), device_id_type=mesh_ids,
        )

    def rims_copy(j, i):
        part = p_all.at[pl.ds(base + i * tiles, tiles)]
        return pltpu.make_async_remote_copy(
            src_ref=part, dst_ref=part, send_sem=p_send.at[j, i], recv_sem=p_recv.at[j, i],
            device_id=peer(j), device_id_type=mesh_ids,
        )

    @pl.when(step == 0)
    def _():
        for j in range(1, tile_size):
            pl.semaphore_signal(barrier, inc=1, device_id=peer(j), device_id_type=mesh_ids)
        x = x_ref[...].reshape(slots * 16, CELLS)
        cols = dot(x, pick_ref[...])
        first = x[:, :LANES].astype(jnp.float32)
        last = pltpu.roll(x[:, CELLS - LANES :].astype(jnp.float32), 2 * TS, 1)
        lane = lax.broadcasted_iota(jnp.int32, (slots * 16, LANES), 1)
        q = jnp.where(lane < TS, first, jnp.where(lane < 2 * TS, last, cols))
        q_all[pl.ds(base, slots)] = q.astype(jnp.bfloat16).reshape(slots, 16, LANES)

    lane = lane_ids(CELLS)
    w = lane % TS
    blk = lane_ids(LANES)

    def rows_added(y):
        up = jnp.where(lane < CELLS - TS, pltpu.roll(y[0], CELLS - TS, 1), 0.0)
        down = jnp.where(lane >= TS, pltpu.roll(y[2], TS, 1), 0.0)
        return y[1] + up + down

    kept, sides = [], []
    for t in range(tiles):
        z = dot(wt_ref[...], g_ref[t])
        rows, rim = [], []
        for a in range(3):
            z0, z1, z2 = (z[(a * 3 + c) * 16 : (a * 3 + c + 1) * 16] for c in range(3))
            rows.append(
                z1
                + jnp.where(w != TS - 1, pltpu.roll(z0, CELLS - 1, 1), 0.0)
                + jnp.where(w != 0, pltpu.roll(z2, 1, 1), 0.0)
            )
            rim.append(jnp.where(w == 0, z0, jnp.where(w == TS - 1, z2, 0.0)))
        inner_ref[t] = rows_added(rows)
        sides.append(rows_added(rim).astype(jnp.bfloat16))
        c0 = rim[0][:, :LANES]
        c2 = rim[2][:, CELLS - LANES :]
        corner = jnp.where(blk == 0, c0, 0.0)
        corner += jnp.where(blk == TS, pltpu.roll(c0, 1, 1), 0.0)
        corner += jnp.where(blk == 2 * TS, pltpu.roll(c2, LANES - TS, 1), 0.0)
        corner += jnp.where(blk == 3 * TS, pltpu.roll(c2, LANES - TS + 1, 1), 0.0)
        kept.append((rows[0][:, :LANES], rows[2][:, CELLS - LANES :], corner))
    cols = dot(jnp.concatenate(sides, axis=0), pick_ref[...])
    for t in range(tiles):
        first, last, corner = kept[t]
        edge = jnp.where(
            blk < TS,
            first,
            jnp.where(blk < 2 * TS, pltpu.roll(last, 2 * TS, 1), cols[t * 16 : (t + 1) * 16]),
        )
        both = jnp.concatenate([edge, corner], axis=1)
        p_all[base + step * tiles + t] = both.astype(jnp.bfloat16)

    @pl.when(step == 0)
    def _():
        pl.semaphore_wait(barrier, tile_size - 1)
        for j in range(1, tile_size):
            edges_copy(j).start()

    for j in range(1, tile_size):
        rims_copy(j, step).start()

    @pl.when(step == steps - 1)
    def _():
        for j in range(1, tile_size):
            edges_copy(j).wait()
            for i in range(steps):
                rims_copy(j, i).wait()
        edges_ref[...] = q_all[...]
        rims_ref[...] = p_all[...]


def front_kernel(
    slots, fsrc_ref, q_ref, var_ref, img_ref, x_ref, g_ref, w_ref, bias_ref,
    out_ref, dw_ref, v_ref, rim_ref, ri_ref, col_ref,
):
    step = pl.program_id(0)
    blk = lane_ids(LANES)

    @pl.when(step == 0)
    def _():
        total = q_ref.shape[0]
        q = q_ref[...].reshape(total * 16, LANES)
        for j in range(8):
            got = dot(q, var_ref[:, j * LANES : (j + 1) * LANES])
            v_ref[j * total : (j + 1) * total] = got.reshape(total, 16, LANES)
        for s in range(slots):
            for half in range(2):
                parts = [v_ref[fsrc_ref[s * 8 + half * 4 + k]] for k in range(4)]
                rim = jnp.where(
                    blk < 2 * TS,
                    jnp.where(blk < TS, parts[0], parts[1]),
                    jnp.where(blk < 3 * TS, parts[2], parts[3]),
                )
                rim_ref[s, :, half * LANES : (half + 1) * LANES] = rim.astype(jnp.bfloat16)
        ri = dot(rim_ref[...].reshape(slots * 16, 2 * LANES), img_ref[...])
        ri_ref[...] = ri.reshape(slots, 16, CELLS + 3 * LANES)
        dw_ref[...] = jnp.zeros_like(dw_ref)
        for t in range(col_ref.shape[0]):
            col_ref[t, 144:160, :] = jnp.ones((16, CELLS), jnp.bfloat16)

    w = lane_ids(CELLS) % TS
    tiles = x_ref.shape[0]
    total = jnp.zeros(dw_ref.shape, jnp.float32)
    for t in range(tiles):
        s = step * tiles + t
        x = x_ref[t].astype(jnp.float32)
        lr = ri_ref[s, :, :CELLS]
        mids = [
            jnp.where(w == 0, lr, pltpu.roll(x, 1, 1)),
            x,
            jnp.where(w == TS - 1, lr, pltpu.roll(x, CELLS - 1, 1)),
        ]
        for c in range(3):
            rim = ri_ref[s, :, CELLS + c * LANES : CELLS + (c + 1) * LANES]
            down = pltpu.roll(mids[c], TS, 1)
            up = pltpu.roll(mids[c], CELLS - TS, 1)
            down = jnp.concatenate(
                [jnp.where(blk < TS, rim, down[:, :LANES]), down[:, LANES:]], axis=1
            )
            up = jnp.concatenate(
                [up[:, : CELLS - LANES], jnp.where(blk >= 3 * TS, rim, up[:, CELLS - LANES :])],
                axis=1,
            )
            for a, tap in enumerate((down, mids[c], up)):
                row = (a * 3 + c) * 16
                col_ref[t, row : row + 16, :] = tap.astype(jnp.bfloat16)
        col = col_ref[t]
        out_ref[t] = (dot(w_ref[...], col[:144]) + bias_ref[...]).astype(jnp.bfloat16)
        total += lax.dot_general(
            g_ref[t], col, (((1,), (1,)), ((), ())), preferred_element_type=jnp.float32
        )
    dw_ref[...] += total


def finish_kernel(slots, bsrc_ref, bdst_ref, p_ref, var_ref, img_ref, inner_ref, out_ref, u_ref, acc_ref, r_ref):
    total = p_ref.shape[0]
    blk = lane_ids(LANES)
    for kind in range(2):
        p = p_ref[:, :, kind * LANES : (kind + 1) * LANES].reshape(total * 16, LANES)
        for j in range(8):
            got = dot(p, var_ref[:, j * LANES : (j + 1) * LANES])
            at = (kind * 8 + j) * total
            u_ref[at : at + total] = got.reshape(total, 16, LANES)
    acc_ref[...] = jnp.zeros_like(acc_ref)

    def add(q, carry):
        for k in range(8):
            d = bdst_ref[q * 8 + k]
            acc_ref[d] = acc_ref[d] + u_ref[bsrc_ref[q * 8 + k]]
        return carry

    lax.fori_loop(0, total, add, 0)
    for s in range(slots):
        parts = [acc_ref[s * 4 + k] for k in range(4)]
        r = jnp.where(
            blk < 2 * TS,
            jnp.where(blk < TS, parts[0], parts[1]),
            jnp.where(blk < 3 * TS, parts[2], parts[3]),
        )
        hi = r.astype(jnp.bfloat16)
        r_ref[s, :, :LANES] = hi
        r_ref[s, :, LANES:] = (r - hi.astype(jnp.float32)).astype(jnp.bfloat16)
    add_in = dot(r_ref[...].reshape(slots * 16, 2 * LANES), img_ref[...])
    out = inner_ref[...].reshape(slots * 16, CELLS) + add_in
    out_ref[...] = out.astype(jnp.bfloat16).reshape(slots, 16, CELLS)


def sum_kernel(dp_size, tile_size, factor, in_ref, out_ref, near_ref, far_ref, near_send, near_recv, far_send, far_recv):
    dp, tile = lax.axis_index("dp"), lax.axis_index("tile")
    pairs = dp_size // 2
    core, hi = lax.rem(dp, 2), dp // 2
    near_count = 2 * tile_size

    def near_peer(j):
        return (hi * 2 + lax.rem(core + j % 2, 2), lax.rem(tile + j // 2, tile_size))

    def far_peer(j):
        return (lax.rem(hi + j, pairs) * 2 + core, tile)

    peers = [near_peer(j) for j in range(1, near_count)] + [far_peer(j) for j in range(1, pairs)]
    barrier = pltpu.get_barrier_semaphore()
    for peer in peers:
        pl.semaphore_signal(barrier, inc=1, device_id=peer, device_id_type=pl.DeviceIdType.MESH)

    rows = in_ref.shape[0]
    quarter = rows // 4
    rest = in_ref[:, LANES:]
    packed = jnp.concatenate(
        [
            in_ref[:, :LANES],
            jnp.concatenate([rest[k * quarter : (k + 1) * quarter] for k in range(4)], axis=1),
        ],
        axis=0,
    )
    pl.semaphore_wait(barrier, len(peers))

    def exchange(value, ref, me, count, peer_of, send, recv):
        ref[me] = value
        copies = []
        for j in range(1, count):
            copy = pltpu.make_async_remote_copy(
                src_ref=ref.at[me],
                dst_ref=ref.at[me],
                send_sem=send.at[j],
                recv_sem=recv.at[j],
                device_id=peer_of(j),
                device_id_type=pl.DeviceIdType.MESH,
            )
            copy.start()
            copies.append(copy)
        for copy in copies:
            copy.wait_recv()
        total = ref[0]
        for j in range(1, count):
            total = total + ref[j]
        return total, copies

    near, near_copies = exchange(
        packed, near_ref, core * tile_size + tile, near_count, near_peer, near_send, near_recv
    )
    far, far_copies = exchange(near, far_ref, hi, pairs, far_peer, far_send, far_recv)
    far = far * factor
    out_ref[:, :LANES] = far[:rows]
    for k in range(4):
        out_ref[k * quarter : (k + 1) * quarter, LANES:] = far[rows:, k * 32 : (k + 1) * 32]
    for copy in near_copies + far_copies:
        copy.wait_send()


def params():
    return pltpu.CompilerParams(vmem_limit_bytes=VMEM_LIMIT)


def cost(flops, bytes_accessed):
    return pl.CostEstimate(flops=flops, bytes_accessed=bytes_accessed, transcendentals=0)


def body(fields, weights, bias, cotangent, neighbours, rotations, tile_map):
    batch_loc, slots, in_chans, cells = fields.shape
    out_chans = weights.shape[0]
    x = fields.reshape(slots, in_chans, cells)
    g = cotangent.reshape(slots, out_chans, cells)
    tiles = 3
    steps = slots // tiles
    f32, bf16 = jnp.float32, jnp.bfloat16
    pick = const(column_picker())
    variants = const(strip_variants())
    vmem = pl.BlockSpec(memory_space=pltpu.VMEM)
    smem = pl.BlockSpec(memory_space=pltpu.SMEM)

    def whole(*dims):
        return pl.BlockSpec(dims, lambda i, *_: (0,) * len(dims))

    def block(*dims):
        return pl.BlockSpec((tiles, *dims), lambda i, *_: (i,) + (0,) * len(dims))

    tile_size, dp_size = lax.axis_size("tile"), lax.axis_size("dp")
    total = tile_size * slots
    wt = weights.transpose(2, 3, 1, 0).reshape(9 * in_chans, out_chans)
    back_tiles = 6
    back_steps = slots // back_tiles
    inner, all_edges, all_rims = pl.pallas_call(
        lambda *refs: gather_kernel(tile_size, *refs),
        grid=(back_steps,),
        out_shape=(
            jax.ShapeDtypeStruct((slots, in_chans, cells), f32),
            jax.ShapeDtypeStruct((total, in_chans, LANES), bf16),
            jax.ShapeDtypeStruct((total, in_chans, 2 * LANES), bf16),
        ),
        in_specs=[
            whole(slots, in_chans, cells),
            pl.BlockSpec((back_tiles, out_chans, cells), lambda i: (i, 0, 0)),
            whole(*wt.shape),
            whole(*pick.shape),
        ],
        out_specs=(
            pl.BlockSpec((back_tiles, in_chans, cells), lambda i: (i, 0, 0)),
            whole(total, in_chans, LANES),
            whole(total, in_chans, 2 * LANES),
        ),
        scratch_shapes=[
            pltpu.VMEM((total, in_chans, LANES), bf16),
            pltpu.VMEM((total, in_chans, 2 * LANES), bf16),
            pltpu.SemaphoreType.DMA((tile_size,)),
            pltpu.SemaphoreType.DMA((tile_size,)),
            pltpu.SemaphoreType.DMA((tile_size, back_steps)),
            pltpu.SemaphoreType.DMA((tile_size, back_steps)),
        ],
        compiler_params=pltpu.CompilerParams(
            collective_id=1, has_side_effects=True, vmem_limit_bytes=VMEM_LIMIT
        ),
        name="back",
    )(x, g, wt, pick)

    slot_nbr, edge_code, flip_code = slot_tables(tile_map, neighbours, rotations)
    base = lax.axis_index("tile") * slots
    src = (edge_code * 2 + flip_code) * total + slot_nbr
    fsrc = lax.dynamic_slice_in_dim(src, base, slots, 0).reshape(-1)
    here = slot_nbr - base
    bdst = jnp.where((here >= 0) & (here < slots), here * 4 + edge_code, slots * 4).reshape(-1)
    ks = jnp.arange(8, dtype=jnp.int32)[None, :]
    bsrc = ((ks * 2 + flip_code) * total + jnp.arange(total, dtype=jnp.int32)[:, None]).reshape(-1)

    wf = weights.transpose(0, 2, 3, 1).reshape(out_chans, 9 * in_chans)
    images = const(rim_images())
    outputs, sums = pl.pallas_call(
        lambda *refs: front_kernel(slots, *refs),
        grid_spec=pltpu.PrefetchScalarGridSpec(
            num_scalar_prefetch=1,
            grid=(steps,),
            in_specs=[
                whole(*all_edges.shape),
                whole(*variants.shape),
                whole(*images.shape),
                block(in_chans, cells),
                block(out_chans, cells),
                whole(*wf.shape),
                whole(out_chans, 1),
            ],
            out_specs=(block(out_chans, cells), whole(out_chans, 160)),
            scratch_shapes=[
                pltpu.VMEM((8 * total, in_chans, LANES), f32),
                pltpu.VMEM((slots, in_chans, 2 * LANES), bf16),
                pltpu.VMEM((slots, in_chans, CELLS + 3 * LANES), f32),
                pltpu.VMEM((tiles, 160, CELLS), bf16),
            ],
        ),
        out_shape=(
            jax.ShapeDtypeStruct((slots, out_chans, cells), bf16),
            jax.ShapeDtypeStruct((out_chans, 160), f32),
        ),
        compiler_params=params(),
        cost_estimate=cost(slots * 1024 * 144 * 256 * 8, slots * 64 * CELLS * 4),
        name="front",
    )(fsrc, all_edges, variants, images, x, g, wf, bias[:, None])
    factor = 1.0 / math.sqrt(
        batch_loc * lax.axis_size("dp") * slots * lax.axis_size("tile") * cells
    )
    packed_rows = out_chans + out_chans // 4
    sums = pl.pallas_call(
        lambda *refs: sum_kernel(dp_size, tile_size, factor, *refs),
        out_shape=jax.ShapeDtypeStruct((out_chans, 160), f32),
        in_specs=[vmem],
        out_specs=vmem,
        scratch_shapes=[
            pltpu.VMEM((2 * tile_size, packed_rows, LANES), f32),
            pltpu.VMEM((dp_size // 2, packed_rows, LANES), f32),
            pltpu.SemaphoreType.DMA((2 * tile_size,)),
            pltpu.SemaphoreType.DMA((2 * tile_size,)),
            pltpu.SemaphoreType.DMA((dp_size // 2,)),
            pltpu.SemaphoreType.DMA((dp_size // 2,)),
        ],
        compiler_params=pltpu.CompilerParams(
            collective_id=0, has_side_effects=True, vmem_limit_bytes=VMEM_LIMIT
        ),
        name="sums",
    )(sums)
    grad_weights = sums[:, :144].reshape(out_chans, 3, 3, in_chans).transpose(0, 3, 1, 2)
    grad_bias = sums[:, 144]

    edge_img = const(edge_images())
    grad_fields = pl.pallas_call(
        lambda *refs: finish_kernel(slots, *refs),
        out_shape=jax.ShapeDtypeStruct((slots, in_chans, cells), bf16),
        in_specs=[smem, smem, vmem, vmem, vmem, vmem],
        out_specs=vmem,
        scratch_shapes=[
            pltpu.VMEM((16 * total, in_chans, LANES), f32),
            pltpu.VMEM((4 * slots + 8, in_chans, LANES), f32),
            pltpu.VMEM((slots, in_chans, 2 * LANES), bf16),
        ],
        compiler_params=params(),
        cost_estimate=cost(slots * 1024 * 144 * 128 * 8, slots * 64 * CELLS * 4),
        name="finish",
    )(bsrc, bdst, all_rims, variants, edge_img, inner)
    return (
        outputs.reshape(cotangent.shape),
        grad_fields.reshape(fields.shape),
        grad_weights,
        grad_bias,
    )


def solution(mesh):
    placed = (P("dp", "tile", None, None), P(), P(), P("dp", "tile", None, None), P(), P(), P())
    return jax.shard_map(
        body,
        mesh=mesh,
        in_specs=placed,
        out_specs=(P("dp", "tile", None, None), P("dp", "tile", None, None), P(), P()),
        check_vma=False,
    )
```

```python
import math

import jax
import jax.numpy as jnp
import numpy as np
from jax import lax
from jax.experimental import pallas as pl
from jax.experimental.pallas import tpu as pltpu
from jax.sharding import PartitionSpec as P

TS = 32


edge_table = np.array(
    [
        [1, 2, 0, 3],
        [0, 3, 1, 2],
        [3, 1, 2, 0],
        [2, 0, 3, 1],
        [1, 1, 0, 0],
        [1, 0, 0, 1],
        [0, 1, 1, 0],
        [0, 0, 1, 1],
    ],
    dtype=np.int32,
)
flip_table = np.array(
    [
        [0, 0, 1, 1],
        [0, 0, 1, 1],
        [0, 1, 1, 0],
        [0, 1, 1, 0],
        [1, 0, 0, 1],
        [0, 0, 1, 1],
        [1, 1, 0, 0],
        [0, 1, 1, 0],
    ],
    dtype=np.int32,
)


def slot_tables(tile_map, neighbours, rotations):
    total_slots = tile_map.shape[0]
    places = jnp.arange(total_slots, dtype=jnp.int32)
    onehot = (tile_map[:, None] == places[None, :]).astype(jnp.int32)
    inverse = jnp.sum(
        (tile_map[None, :] == places[:, None]).astype(jnp.int32) * places[None, :], axis=1
    )
    tile_nbr = jnp.sum(onehot[:, :, None] * neighbours[None], axis=1)
    tile_rot = jnp.sum(onehot[:, :, None] * rotations[None], axis=1)
    slot_nbr = jnp.sum(
        (tile_nbr[:, :, None] == places[None, None, :]).astype(jnp.int32) * inverse[None, None, :],
        axis=2,
    )
    matches = (tile_rot[:, :, None] == jnp.arange(4, dtype=jnp.int32)).astype(jnp.int32)
    edge_code = jnp.sum(matches * jnp.asarray(edge_table)[None], axis=-1)
    flip_code = jnp.sum(matches * jnp.asarray(flip_table)[None], axis=-1)
    return (slot_nbr, edge_code, flip_code)


CELLS = TS * TS
LANES = 128
VMEM_LIMIT = 50 * 1024 * 1024


def column_picker():
    m = np.zeros((CELLS, LANES), np.float32)
    for h in range(TS):
        m[h * TS, 2 * TS + h] = 1
        m[h * TS + TS - 1, 3 * TS + h] = 1
    return m


def strip_variants():
    m = np.zeros((LANES, 8 * LANES), np.float32)
    for edge in range(4):
        for flip in range(2):
            for rep in range(4):
                for t in range(TS):
                    at = TS - 1 - t if flip else t
                    m[edge * TS + at, (edge * 2 + flip) * LANES + rep * TS + t] = 1
    return m


def rim_images():
    m = np.zeros((2 * LANES, CELLS + 3 * LANES), np.float32)
    for h in range(TS):
        m[2 * TS + h, h * TS] = 1
        m[3 * TS + h, h * TS + TS - 1] = 1
    tops = [LANES] + list(range(TS)) + [LANES + TS]
    lows = [LANES + 2 * TS] + list(range(TS, 2 * TS)) + [LANES + 3 * TS]
    for col_tap in range(3):
        for w in range(TS):
            m[tops[w + col_tap], CELLS + col_tap * LANES + w] = 1
            m[lows[w + col_tap], CELLS + col_tap * LANES + 3 * TS + w] = 1
    return m


def edge_images():
    m = np.zeros((LANES, CELLS), np.float32)
    for t in range(TS):
        m[t, t] = 1
        m[TS + t, (TS - 1) * TS + t] = 1
        m[2 * TS + t, t * TS] = 1
        m[3 * TS + t, t * TS + TS - 1] = 1
    return np.concatenate([m, m], axis=0)


def const(m):
    return jnp.asarray(m.astype(jnp.bfloat16))


def dot(a, b):
    return jnp.dot(a, b, preferred_element_type=jnp.float32)


def lane_ids(width):
    return lax.broadcasted_iota(jnp.int32, (16, width), 1)


def gather_kernel(
    tile_size, x_ref, g_ref, wt_ref, pick_ref, inner_ref, edges_ref, rims_ref,
    q_all, p_all, q_send, q_recv, p_send, p_recv,
):
    step = pl.program_id(0)
    slots, tiles = x_ref.shape[0], g_ref.shape[0]
    steps = slots // tiles
    dp, tile = lax.axis_index("dp"), lax.axis_index("tile")
    base = tile * slots
    barrier = pltpu.get_barrier_semaphore()
    mesh_ids = pl.DeviceIdType.MESH

    def peer(j):
        return (dp, lax.rem(tile + j, tile_size))

    def edges_copy(j):
        part = q_all.at[pl.ds(base, slots)]
        return pltpu.make_async_remote_copy(
            src_ref=part, dst_ref=part, send_sem=q_send.at[j], recv_sem=q_recv.at[j],
            device_id=peer(j), device_id_type=mesh_ids,
        )

    def rims_copy(j, i):
        part = p_all.at[pl.ds(base + i * tiles, tiles)]
        return pltpu.make_async_remote_copy(
            src_ref=part, dst_ref=part, send_sem=p_send.at[j, i], recv_sem=p_recv.at[j, i],
            device_id=peer(j), device_id_type=mesh_ids,
        )

    @pl.when(step == 0)
    def _():
        for j in range(1, tile_size):
            pl.semaphore_signal(barrier, inc=1, device_id=peer(j), device_id_type=mesh_ids)
        x = x_ref[...].reshape(slots * 16, CELLS)
        cols = dot(x, pick_ref[...])
        first = x[:, :LANES].astype(jnp.float32)
        last = pltpu.roll(x[:, CELLS - LANES :].astype(jnp.float32), 2 * TS, 1)
        lane = lax.broadcasted_iota(jnp.int32, (slots * 16, LANES), 1)
        q = jnp.where(lane < TS, first, jnp.where(lane < 2 * TS, last, cols))
        q_all[pl.ds(base, slots)] = q.astype(jnp.bfloat16).reshape(slots, 16, LANES)

    lane = lane_ids(CELLS)
    w = lane % TS
    blk = lane_ids(LANES)

    def rows_added(y):
        up = jnp.where(lane < CELLS - TS, pltpu.roll(y[0], CELLS - TS, 1), 0.0)
        down = jnp.where(lane >= TS, pltpu.roll(y[2], TS, 1), 0.0)
        return y[1] + up + down

    kept, sides = [], []
    for t in range(tiles):
        z = dot(wt_ref[...], g_ref[t])
        rows, rim = [], []
        for a in range(3):
            z0, z1, z2 = (z[(a * 3 + c) * 16 : (a * 3 + c + 1) * 16] for c in range(3))
            rows.append(
                z1
                + jnp.where(w != TS - 1, pltpu.roll(z0, CELLS - 1, 1), 0.0)
                + jnp.where(w != 0, pltpu.roll(z2, 1, 1), 0.0)
            )
            rim.append(jnp.where(w == 0, z0, jnp.where(w == TS - 1, z2, 0.0)))
        inner_ref[t] = rows_added(rows)
        sides.append(rows_added(rim).astype(jnp.bfloat16))
        c0 = rim[0][:, :LANES]
        c2 = rim[2][:, CELLS - LANES :]
        corner = jnp.where(blk == 0, c0, 0.0)
        corner += jnp.where(blk == TS, pltpu.roll(c0, 1, 1), 0.0)
        corner += jnp.where(blk == 2 * TS, pltpu.roll(c2, LANES - TS, 1), 0.0)
        corner += jnp.where(blk == 3 * TS, pltpu.roll(c2, LANES - TS + 1, 1), 0.0)
        kept.append((rows[0][:, :LANES], rows[2][:, CELLS - LANES :], corner))
    cols = dot(jnp.concatenate(sides, axis=0), pick_ref[...])
    for t in range(tiles):
        first, last, corner = kept[t]
        edge = jnp.where(
            blk < TS,
            first,
            jnp.where(blk < 2 * TS, pltpu.roll(last, 2 * TS, 1), cols[t * 16 : (t + 1) * 16]),
        )
        both = jnp.concatenate([edge, corner], axis=1)
        p_all[base + step * tiles + t] = both.astype(jnp.bfloat16)

    @pl.when(step == 0)
    def _():
        pl.semaphore_wait(barrier, tile_size - 1)
        for j in range(1, tile_size):
            edges_copy(j).start()

    for j in range(1, tile_size):
        rims_copy(j, step).start()

    @pl.when(step == steps - 1)
    def _():
        for j in range(1, tile_size):
            edges_copy(j).wait()
            for i in range(steps):
                rims_copy(j, i).wait()
        edges_ref[...] = q_all[...]
        rims_ref[...] = p_all[...]


def front_kernel(
    slots, fsrc_ref, q_ref, var_ref, img_ref, x_ref, g_ref, w_ref, bias_ref,
    out_ref, dw_ref, v_ref, rim_ref, ri_ref, col_ref,
):
    step = pl.program_id(0)
    blk = lane_ids(LANES)

    @pl.when(step == 0)
    def _():
        total = q_ref.shape[0]
        q = q_ref[...].reshape(total * 16, LANES)
        for j in range(8):
            got = dot(q, var_ref[:, j * LANES : (j + 1) * LANES])
            v_ref[j * total : (j + 1) * total] = got.reshape(total, 16, LANES)
        for s in range(slots):
            for half in range(2):
                parts = [v_ref[fsrc_ref[s * 8 + half * 4 + k]] for k in range(4)]
                rim = jnp.where(
                    blk < 2 * TS,
                    jnp.where(blk < TS, parts[0], parts[1]),
                    jnp.where(blk < 3 * TS, parts[2], parts[3]),
                )
                rim_ref[s, :, half * LANES : (half + 1) * LANES] = rim.astype(jnp.bfloat16)
        ri = dot(rim_ref[...].reshape(slots * 16, 2 * LANES), img_ref[...])
        ri_ref[...] = ri.reshape(slots, 16, CELLS + 3 * LANES)
        dw_ref[...] = jnp.zeros_like(dw_ref)
        for t in range(col_ref.shape[0]):
            col_ref[t, 144:160, :] = jnp.ones((16, CELLS), jnp.bfloat16)

    w = lane_ids(CELLS) % TS
    tiles = x_ref.shape[0]
    total = jnp.zeros(dw_ref.shape, jnp.float32)
    for t in range(tiles):
        s = step * tiles + t
        x = x_ref[t].astype(jnp.float32)
        lr = ri_ref[s, :, :CELLS]
        mids = [
            jnp.where(w == 0, lr, pltpu.roll(x, 1, 1)),
            x,
            jnp.where(w == TS - 1, lr, pltpu.roll(x, CELLS - 1, 1)),
        ]
        for c in range(3):
            rim = ri_ref[s, :, CELLS + c * LANES : CELLS + (c + 1) * LANES]
            down = pltpu.roll(mids[c], TS, 1)
            up = pltpu.roll(mids[c], CELLS - TS, 1)
            down = jnp.concatenate(
                [jnp.where(blk < TS, rim, down[:, :LANES]), down[:, LANES:]], axis=1
            )
            up = jnp.concatenate(
                [up[:, : CELLS - LANES], jnp.where(blk >= 3 * TS, rim, up[:, CELLS - LANES :])],
                axis=1,
            )
            for a, tap in enumerate((down, mids[c], up)):
                row = (a * 3 + c) * 16
                col_ref[t, row : row + 16, :] = tap.astype(jnp.bfloat16)
        col = col_ref[t]
        out_ref[t] = (dot(w_ref[...], col[:144]) + bias_ref[...]).astype(jnp.bfloat16)
        total += lax.dot_general(
            g_ref[t], col, (((1,), (1,)), ((), ())), preferred_element_type=jnp.float32
        )
    dw_ref[...] += total


def finish_kernel(slots, bsrc_ref, bdst_ref, p_ref, var_ref, img_ref, inner_ref, out_ref, u_ref, acc_ref, r_ref):
    total = p_ref.shape[0]
    blk = lane_ids(LANES)
    for kind in range(2):
        p = p_ref[:, :, kind * LANES : (kind + 1) * LANES].reshape(total * 16, LANES)
        for j in range(8):
            got = dot(p, var_ref[:, j * LANES : (j + 1) * LANES])
            at = (kind * 8 + j) * total
            u_ref[at : at + total] = got.reshape(total, 16, LANES)
    acc_ref[...] = jnp.zeros_like(acc_ref)

    def add(q, carry):
        for k in range(8):
            d = bdst_ref[q * 8 + k]
            acc_ref[d] = acc_ref[d] + u_ref[bsrc_ref[q * 8 + k]]
        return carry

    lax.fori_loop(0, total, add, 0)
    for s in range(slots):
        parts = [acc_ref[s * 4 + k] for k in range(4)]
        r = jnp.where(
            blk < 2 * TS,
            jnp.where(blk < TS, parts[0], parts[1]),
            jnp.where(blk < 3 * TS, parts[2], parts[3]),
        )
        hi = r.astype(jnp.bfloat16)
        r_ref[s, :, :LANES] = hi
        r_ref[s, :, LANES:] = (r - hi.astype(jnp.float32)).astype(jnp.bfloat16)
    add_in = dot(r_ref[...].reshape(slots * 16, 2 * LANES), img_ref[...])
    out = inner_ref[...].reshape(slots * 16, CELLS) + add_in
    out_ref[...] = out.astype(jnp.bfloat16).reshape(slots, 16, CELLS)


def sum_kernel(
    dp_size, tile_size, factor, in_ref, out_ref, src_ref, near_ref, far_ref, all_ref,
    near_send, near_recv, far_send, far_recv, all_send, all_recv,
):
    dp, tile = lax.axis_index("dp"), lax.axis_index("tile")
    pairs = dp_size // 2
    core, hi = lax.rem(dp, 2), dp // 2
    near_count = 2 * tile_size
    chunk = src_ref.shape[1]
    me = core * tile_size + tile
    mesh_ids = pl.DeviceIdType.MESH

    def near_peer(j):
        return (lax.rem(core + j % 2, 2), lax.rem(tile + j // 2, tile_size))

    def near_device(j):
        peer_core, peer_tile = near_peer(j)
        return (hi * 2 + peer_core, peer_tile)

    def far_device(j):
        return (lax.rem(hi + j, pairs) * 2 + core, tile)

    peers = [near_device(j) for j in range(1, near_count)] + [far_device(j) for j in range(1, pairs)]
    barrier = pltpu.get_barrier_semaphore()
    for peer in peers:
        pl.semaphore_signal(barrier, inc=1, device_id=peer, device_id_type=mesh_ids)

    rows = in_ref.shape[0]
    quarter = rows // 4
    rest = in_ref[:, LANES:]
    packed = jnp.concatenate(
        [
            in_ref[:, :LANES],
            jnp.concatenate([rest[k * quarter : (k + 1) * quarter] for k in range(4)], axis=1),
            jnp.zeros((near_count * chunk - rows - quarter, LANES), jnp.float32),
        ],
        axis=0,
    )
    src_ref[...] = packed.reshape(near_count, chunk, LANES)
    near_ref[me] = src_ref[me]
    pl.semaphore_wait(barrier, len(peers))

    def exchange(count, src_of, dst, device_of, send, recv):
        copies = []
        for j in range(1, count):
            copy = pltpu.make_async_remote_copy(
                src_ref=src_of(j),
                dst_ref=dst,
                send_sem=send.at[j],
                recv_sem=recv.at[j],
                device_id=device_of(j),
                device_id_type=mesh_ids,
            )
            copy.start()
            copies.append(copy)
        for copy in copies:
            copy.wait_recv()
        return copies

    def added(ref):
        total = ref[0]
        for j in range(1, ref.shape[0]):
            total = total + ref[j]
        return total

    def chunk_for(j):
        peer_core, peer_tile = near_peer(j)
        return src_ref.at[peer_core * tile_size + peer_tile]

    copies = exchange(near_count, chunk_for, near_ref.at[me], near_device, near_send, near_recv)
    far_ref[hi] = added(near_ref)
    copies += exchange(
        pairs, lambda j: far_ref.at[hi], far_ref.at[hi], far_device, far_send, far_recv
    )
    all_ref[me] = added(far_ref) * factor
    copies += exchange(
        near_count, lambda j: all_ref.at[me], all_ref.at[me], near_device, all_send, all_recv
    )
    whole = all_ref[...].reshape(near_count * chunk, LANES)
    out_ref[:, :LANES] = whole[:rows]
    for k in range(4):
        out_ref[k * quarter : (k + 1) * quarter, LANES:] = whole[
            rows : rows + quarter, k * 32 : (k + 1) * 32
        ]
    for copy in copies:
        copy.wait_send()


def params():
    return pltpu.CompilerParams(vmem_limit_bytes=VMEM_LIMIT)


def cost(flops, bytes_accessed):
    return pl.CostEstimate(flops=flops, bytes_accessed=bytes_accessed, transcendentals=0)


def body(fields, weights, bias, cotangent, neighbours, rotations, tile_map):
    batch_loc, slots, in_chans, cells = fields.shape
    out_chans = weights.shape[0]
    x = fields.reshape(slots, in_chans, cells)
    g = cotangent.reshape(slots, out_chans, cells)
    tiles = 3
    steps = slots // tiles
    f32, bf16 = jnp.float32, jnp.bfloat16
    pick = const(column_picker())
    variants = const(strip_variants())
    vmem = pl.BlockSpec(memory_space=pltpu.VMEM)
    smem = pl.BlockSpec(memory_space=pltpu.SMEM)

    def whole(*dims):
        return pl.BlockSpec(dims, lambda i, *_: (0,) * len(dims))

    def block(*dims):
        return pl.BlockSpec((tiles, *dims), lambda i, *_: (i,) + (0,) * len(dims))

    tile_size, dp_size = lax.axis_size("tile"), lax.axis_size("dp")
    total = tile_size * slots
    wt = weights.transpose(2, 3, 1, 0).reshape(9 * in_chans, out_chans)
    back_tiles = 6
    back_steps = slots // back_tiles
    inner, all_edges, all_rims = pl.pallas_call(
        lambda *refs: gather_kernel(tile_size, *refs),
        grid=(back_steps,),
        out_shape=(
            jax.ShapeDtypeStruct((slots, in_chans, cells), f32),
            jax.ShapeDtypeStruct((total, in_chans, LANES), bf16),
            jax.ShapeDtypeStruct((total, in_chans, 2 * LANES), bf16),
        ),
        in_specs=[
            whole(slots, in_chans, cells),
            pl.BlockSpec((back_tiles, out_chans, cells), lambda i: (i, 0, 0)),
            whole(*wt.shape),
            whole(*pick.shape),
        ],
        out_specs=(
            pl.BlockSpec((back_tiles, in_chans, cells), lambda i: (i, 0, 0)),
            whole(total, in_chans, LANES),
            whole(total, in_chans, 2 * LANES),
        ),
        scratch_shapes=[
            pltpu.VMEM((total, in_chans, LANES), bf16),
            pltpu.VMEM((total, in_chans, 2 * LANES), bf16),
            pltpu.SemaphoreType.DMA((tile_size,)),
            pltpu.SemaphoreType.DMA((tile_size,)),
            pltpu.SemaphoreType.DMA((tile_size, back_steps)),
            pltpu.SemaphoreType.DMA((tile_size, back_steps)),
        ],
        compiler_params=pltpu.CompilerParams(
            collective_id=1, has_side_effects=True, vmem_limit_bytes=VMEM_LIMIT
        ),
        name="back",
    )(x, g, wt, pick)

    slot_nbr, edge_code, flip_code = slot_tables(tile_map, neighbours, rotations)
    base = lax.axis_index("tile") * slots
    src = (edge_code * 2 + flip_code) * total + slot_nbr
    fsrc = lax.dynamic_slice_in_dim(src, base, slots, 0).reshape(-1)
    here = slot_nbr - base
    bdst = jnp.where((here >= 0) & (here < slots), here * 4 + edge_code, slots * 4).reshape(-1)
    ks = jnp.arange(8, dtype=jnp.int32)[None, :]
    bsrc = ((ks * 2 + flip_code) * total + jnp.arange(total, dtype=jnp.int32)[:, None]).reshape(-1)

    wf = weights.transpose(0, 2, 3, 1).reshape(out_chans, 9 * in_chans)
    images = const(rim_images())
    outputs, sums = pl.pallas_call(
        lambda *refs: front_kernel(slots, *refs),
        grid_spec=pltpu.PrefetchScalarGridSpec(
            num_scalar_prefetch=1,
            grid=(steps,),
            in_specs=[
                whole(*all_edges.shape),
                whole(*variants.shape),
                whole(*images.shape),
                block(in_chans, cells),
                block(out_chans, cells),
                whole(*wf.shape),
                whole(out_chans, 1),
            ],
            out_specs=(block(out_chans, cells), whole(out_chans, 160)),
            scratch_shapes=[
                pltpu.VMEM((8 * total, in_chans, LANES), f32),
                pltpu.VMEM((slots, in_chans, 2 * LANES), bf16),
                pltpu.VMEM((slots, in_chans, CELLS + 3 * LANES), f32),
                pltpu.VMEM((tiles, 160, CELLS), bf16),
            ],
        ),
        out_shape=(
            jax.ShapeDtypeStruct((slots, out_chans, cells), bf16),
            jax.ShapeDtypeStruct((out_chans, 160), f32),
        ),
        compiler_params=params(),
        cost_estimate=cost(slots * 1024 * 144 * 256 * 8, slots * 64 * CELLS * 4),
        name="front",
    )(fsrc, all_edges, variants, images, x, g, wf, bias[:, None])
    factor = 1.0 / math.sqrt(
        batch_loc * lax.axis_size("dp") * slots * lax.axis_size("tile") * cells
    )
    near_count, pairs = 2 * tile_size, dp_size // 2
    packed_rows = out_chans + out_chans // 4
    chunk = -(-packed_rows // (8 * near_count)) * 8
    sums = pl.pallas_call(
        lambda *refs: sum_kernel(dp_size, tile_size, factor, *refs),
        out_shape=jax.ShapeDtypeStruct((out_chans, 160), f32),
        in_specs=[vmem],
        out_specs=vmem,
        scratch_shapes=[
            pltpu.VMEM((near_count, chunk, LANES), f32),
            pltpu.VMEM((near_count, chunk, LANES), f32),
            pltpu.VMEM((pairs, chunk, LANES), f32),
            pltpu.VMEM((near_count, chunk, LANES), f32),
            pltpu.SemaphoreType.DMA((near_count,)),
            pltpu.SemaphoreType.DMA((near_count,)),
            pltpu.SemaphoreType.DMA((pairs,)),
            pltpu.SemaphoreType.DMA((pairs,)),
            pltpu.SemaphoreType.DMA((near_count,)),
            pltpu.SemaphoreType.DMA((near_count,)),
        ],
        compiler_params=pltpu.CompilerParams(
            collective_id=0, has_side_effects=True, vmem_limit_bytes=VMEM_LIMIT
        ),
        name="sums",
    )(sums)
    grad_weights = sums[:, :144].reshape(out_chans, 3, 3, in_chans).transpose(0, 3, 1, 2)
    grad_bias = sums[:, 144]

    edge_img = const(edge_images())
    grad_fields = pl.pallas_call(
        lambda *refs: finish_kernel(slots, *refs),
        out_shape=jax.ShapeDtypeStruct((slots, in_chans, cells), bf16),
        in_specs=[smem, smem, vmem, vmem, vmem, vmem],
        out_specs=vmem,
        scratch_shapes=[
            pltpu.VMEM((16 * total, in_chans, LANES), f32),
            pltpu.VMEM((4 * slots + 8, in_chans, LANES), f32),
            pltpu.VMEM((slots, in_chans, 2 * LANES), bf16),
        ],
        compiler_params=params(),
        cost_estimate=cost(slots * 1024 * 144 * 128 * 8, slots * 64 * CELLS * 4),
        name="finish",
    )(bsrc, bdst, all_rims, variants, edge_img, inner)
    return (
        outputs.reshape(cotangent.shape),
        grad_fields.reshape(fields.shape),
        grad_weights,
        grad_bias,
    )


def solution(mesh):
    placed = (P("dp", "tile", None, None), P(), P(), P("dp", "tile", None, None), P(), P(), P())
    return jax.shard_map(
        body,
        mesh=mesh,
        in_specs=placed,
        out_specs=(P("dp", "tile", None, None), P("dp", "tile", None, None), P(), P()),
        check_vma=False,
    )
```

```python
import math

import jax
import jax.numpy as jnp
import numpy as np
from jax import lax
from jax.experimental import pallas as pl
from jax.experimental.pallas import tpu as pltpu
from jax.sharding import PartitionSpec as P

TS = 32


edge_table = np.array(
    [
        [1, 2, 0, 3],
        [0, 3, 1, 2],
        [3, 1, 2, 0],
        [2, 0, 3, 1],
        [1, 1, 0, 0],
        [1, 0, 0, 1],
        [0, 1, 1, 0],
        [0, 0, 1, 1],
    ],
    dtype=np.int32,
)
flip_table = np.array(
    [
        [0, 0, 1, 1],
        [0, 0, 1, 1],
        [0, 1, 1, 0],
        [0, 1, 1, 0],
        [1, 0, 0, 1],
        [0, 0, 1, 1],
        [1, 1, 0, 0],
        [0, 1, 1, 0],
    ],
    dtype=np.int32,
)


def tables_kernel(slots, map_ref, nbr_ref, rot_ref, fsrc_ref, bsrc_ref, bdst_ref):
    total = map_ref.shape[1]
    base = lax.axis_index("tile") * slots
    held = map_ref[...].astype(jnp.float32)
    rows = lax.broadcasted_iota(jnp.int32, (total, total), 0)
    cols = lax.broadcasted_iota(jnp.int32, (total, total), 1)
    places = cols.astype(jnp.float32)
    held_col = jnp.sum(jnp.where(rows == cols, held, 0.0), axis=1, keepdims=True)
    onehot = jnp.where(held_col == places, 1.0, 0.0).astype(jnp.bfloat16)
    tile_nbr = dot(onehot, nbr_ref[...].astype(jnp.float32).astype(jnp.bfloat16))
    tile_rot = dot(onehot, rot_ref[...].astype(jnp.float32).astype(jnp.bfloat16))
    k_ids = lax.broadcasted_iota(jnp.int32, (total, 8), 1)
    s_ids = lax.broadcasted_iota(jnp.int32, (total, 8), 0)
    nbr = jnp.zeros((total, 8), jnp.float32)
    edge = jnp.zeros((total, 8), jnp.int32)
    flip = jnp.zeros((total, 8), jnp.int32)
    for k in range(8):
        found = jnp.where(held == tile_nbr[:, k : k + 1], places, 0.0)
        nbr = jnp.where(k_ids == k, jnp.sum(found, axis=1, keepdims=True), nbr)
        for r in range(4):
            here = (k_ids == k) & (tile_rot == float(r))
            edge = jnp.where(here, int(edge_table[k, r]), edge)
            flip = jnp.where(here, int(flip_table[k, r]), flip)
    nbr = nbr.astype(jnp.int32)
    fsrc_ref[...] = (edge * 2 + flip) * total + nbr
    bsrc_ref[...] = (k_ids * 2 + flip) * total + s_ids
    own = nbr - base
    bdst_ref[...] = jnp.where((own >= 0) & (own < slots), own * 4 + edge, slots * 4)


CELLS = TS * TS
LANES = 128
VMEM_LIMIT = 50 * 1024 * 1024


def column_picker():
    m = np.zeros((CELLS, LANES), np.float32)
    for h in range(TS):
        m[h * TS, 2 * TS + h] = 1
        m[h * TS + TS - 1, 3 * TS + h] = 1
    return m


def strip_variants():
    m = np.zeros((LANES, 8 * LANES), np.float32)
    for edge in range(4):
        for flip in range(2):
            for rep in range(4):
                for t in range(TS):
                    at = TS - 1 - t if flip else t
                    m[edge * TS + at, (edge * 2 + flip) * LANES + rep * TS + t] = 1
    return m


def rim_images():
    m = np.zeros((2 * LANES, CELLS + 3 * LANES), np.float32)
    for h in range(TS):
        m[2 * TS + h, h * TS] = 1
        m[3 * TS + h, h * TS + TS - 1] = 1
    tops = [LANES] + list(range(TS)) + [LANES + TS]
    lows = [LANES + 2 * TS] + list(range(TS, 2 * TS)) + [LANES + 3 * TS]
    for col_tap in range(3):
        for w in range(TS):
            m[tops[w + col_tap], CELLS + col_tap * LANES + w] = 1
            m[lows[w + col_tap], CELLS + col_tap * LANES + 3 * TS + w] = 1
    return m


def edge_images():
    m = np.zeros((LANES, CELLS), np.float32)
    for t in range(TS):
        m[t, t] = 1
        m[TS + t, (TS - 1) * TS + t] = 1
        m[2 * TS + t, t * TS] = 1
        m[3 * TS + t, t * TS + TS - 1] = 1
    return np.concatenate([m, m], axis=0)


def const(m):
    return jnp.asarray(m.astype(jnp.bfloat16))


def dot(a, b):
    return jnp.dot(a, b, preferred_element_type=jnp.float32)


def lane_ids(width):
    return lax.broadcasted_iota(jnp.int32, (16, width), 1)


def gather_kernel(
    tile_size, x_ref, g_ref, wt_ref, pick_ref, inner_ref, edges_ref, rims_ref,
    q_all, p_all, q_send, q_recv, p_send, p_recv,
):
    step = pl.program_id(0)
    slots, tiles = x_ref.shape[0], g_ref.shape[0]
    steps = slots // tiles
    dp, tile = lax.axis_index("dp"), lax.axis_index("tile")
    base = tile * slots
    barrier = pltpu.get_barrier_semaphore()
    mesh_ids = pl.DeviceIdType.MESH

    def peer(j):
        return (dp, lax.rem(tile + j, tile_size))

    def edges_copy(j):
        part = q_all.at[pl.ds(base, slots)]
        return pltpu.make_async_remote_copy(
            src_ref=part, dst_ref=part, send_sem=q_send.at[j], recv_sem=q_recv.at[j],
            device_id=peer(j), device_id_type=mesh_ids,
        )

    def rims_copy(j, i):
        part = p_all.at[pl.ds(base + i * tiles, tiles)]
        return pltpu.make_async_remote_copy(
            src_ref=part, dst_ref=part, send_sem=p_send.at[j, i], recv_sem=p_recv.at[j, i],
            device_id=peer(j), device_id_type=mesh_ids,
        )

    @pl.when(step == 0)
    def _():
        for j in range(1, tile_size):
            pl.semaphore_signal(barrier, inc=1, device_id=peer(j), device_id_type=mesh_ids)
        x = x_ref[...].reshape(slots * 16, CELLS)
        cols = dot(x, pick_ref[...])
        first = x[:, :LANES].astype(jnp.float32)
        last = pltpu.roll(x[:, CELLS - LANES :].astype(jnp.float32), 2 * TS, 1)
        lane = lax.broadcasted_iota(jnp.int32, (slots * 16, LANES), 1)
        q = jnp.where(lane < TS, first, jnp.where(lane < 2 * TS, last, cols))
        q_all[pl.ds(base, slots)] = q.astype(jnp.bfloat16).reshape(slots, 16, LANES)

    lane = lane_ids(CELLS)
    w = lane % TS
    blk = lane_ids(LANES)

    def rows_added(y):
        up = jnp.where(lane < CELLS - TS, pltpu.roll(y[0], CELLS - TS, 1), 0.0)
        down = jnp.where(lane >= TS, pltpu.roll(y[2], TS, 1), 0.0)
        return y[1] + up + down

    kept, sides = [], []
    for t in range(tiles):
        z = dot(wt_ref[...], g_ref[t])
        rows, rim = [], []
        for a in range(3):
            z0, z1, z2 = (z[(a * 3 + c) * 16 : (a * 3 + c + 1) * 16] for c in range(3))
            rows.append(
                z1
                + jnp.where(w != TS - 1, pltpu.roll(z0, CELLS - 1, 1), 0.0)
                + jnp.where(w != 0, pltpu.roll(z2, 1, 1), 0.0)
            )
            rim.append(jnp.where(w == 0, z0, jnp.where(w == TS - 1, z2, 0.0)))
        inner_ref[t] = rows_added(rows)
        sides.append(rows_added(rim).astype(jnp.bfloat16))
        c0 = rim[0][:, :LANES]
        c2 = rim[2][:, CELLS - LANES :]
        corner = jnp.where(blk == 0, c0, 0.0)
        corner += jnp.where(blk == TS, pltpu.roll(c0, 1, 1), 0.0)
        corner += jnp.where(blk == 2 * TS, pltpu.roll(c2, LANES - TS, 1), 0.0)
        corner += jnp.where(blk == 3 * TS, pltpu.roll(c2, LANES - TS + 1, 1), 0.0)
        kept.append((rows[0][:, :LANES], rows[2][:, CELLS - LANES :], corner))
    cols = dot(jnp.concatenate(sides, axis=0), pick_ref[...])
    for t in range(tiles):
        first, last, corner = kept[t]
        edge = jnp.where(
            blk < TS,
            first,
            jnp.where(blk < 2 * TS, pltpu.roll(last, 2 * TS, 1), cols[t * 16 : (t + 1) * 16]),
        )
        both = jnp.concatenate([edge, corner], axis=1)
        p_all[base + step * tiles + t] = both.astype(jnp.bfloat16)

    @pl.when(step == 0)
    def _():
        pl.semaphore_wait(barrier, tile_size - 1)
        for j in range(1, tile_size):
            edges_copy(j).start()

    for j in range(1, tile_size):
        rims_copy(j, step).start()

    @pl.when(step == steps - 1)
    def _():
        for j in range(1, tile_size):
            edges_copy(j).wait()
            for i in range(steps):
                rims_copy(j, i).wait()
        edges_ref[...] = q_all[...]
        rims_ref[...] = p_all[...]


def front_kernel(
    slots, fsrc_ref, q_ref, var_ref, img_ref, x_ref, g_ref, w_ref, bias_ref,
    out_ref, dw_ref, v_ref, rim_ref, ri_ref, col_ref,
):
    step = pl.program_id(0)
    blk = lane_ids(LANES)

    @pl.when(step == 0)
    def _():
        total = q_ref.shape[0]
        base = lax.axis_index("tile") * slots
        q = q_ref[...].reshape(total * 16, LANES)
        for j in range(8):
            got = dot(q, var_ref[:, j * LANES : (j + 1) * LANES])
            v_ref[j * total : (j + 1) * total] = got.reshape(total, 16, LANES)
        for s in range(slots):
            for half in range(2):
                parts = [v_ref[fsrc_ref[base + s, half * 4 + k]] for k in range(4)]
                rim = jnp.where(
                    blk < 2 * TS,
                    jnp.where(blk < TS, parts[0], parts[1]),
                    jnp.where(blk < 3 * TS, parts[2], parts[3]),
                )
                rim_ref[s, :, half * LANES : (half + 1) * LANES] = rim.astype(jnp.bfloat16)
        ri = dot(rim_ref[...].reshape(slots * 16, 2 * LANES), img_ref[...])
        ri_ref[...] = ri.reshape(slots, 16, CELLS + 3 * LANES)
        dw_ref[...] = jnp.zeros_like(dw_ref)
        for t in range(col_ref.shape[0]):
            col_ref[t, 144:160, :] = jnp.ones((16, CELLS), jnp.bfloat16)

    w = lane_ids(CELLS) % TS
    tiles = x_ref.shape[0]
    chans = bias_ref.shape[1]
    same = lax.broadcasted_iota(jnp.int32, (chans, chans), 0) == lax.broadcasted_iota(
        jnp.int32, (chans, chans), 1
    )
    bias = jnp.sum(jnp.where(same, bias_ref[...], 0.0), axis=1, keepdims=True)
    total = jnp.zeros(dw_ref.shape, jnp.float32)
    for t in range(tiles):
        s = step * tiles + t
        x = x_ref[t].astype(jnp.float32)
        lr = ri_ref[s, :, :CELLS]
        mids = [
            jnp.where(w == 0, lr, pltpu.roll(x, 1, 1)),
            x,
            jnp.where(w == TS - 1, lr, pltpu.roll(x, CELLS - 1, 1)),
        ]
        for c in range(3):
            rim = ri_ref[s, :, CELLS + c * LANES : CELLS + (c + 1) * LANES]
            down = pltpu.roll(mids[c], TS, 1)
            up = pltpu.roll(mids[c], CELLS - TS, 1)
            down = jnp.concatenate(
                [jnp.where(blk < TS, rim, down[:, :LANES]), down[:, LANES:]], axis=1
            )
            up = jnp.concatenate(
                [up[:, : CELLS - LANES], jnp.where(blk >= 3 * TS, rim, up[:, CELLS - LANES :])],
                axis=1,
            )
            for a, tap in enumerate((down, mids[c], up)):
                row = (a * 3 + c) * 16
                col_ref[t, row : row + 16, :] = tap.astype(jnp.bfloat16)
        col = col_ref[t]
        out_ref[t] = (dot(w_ref[...], col[:144]) + bias).astype(jnp.bfloat16)
        total += lax.dot_general(
            g_ref[t], col, (((1,), (1,)), ((), ())), preferred_element_type=jnp.float32
        )
    dw_ref[...] += total


def finish_kernel(slots, bsrc_ref, bdst_ref, p_ref, var_ref, img_ref, inner_ref, out_ref, u_ref, acc_ref, r_ref):
    total = p_ref.shape[0]
    blk = lane_ids(LANES)
    for kind in range(2):
        p = p_ref[:, :, kind * LANES : (kind + 1) * LANES].reshape(total * 16, LANES)
        for j in range(8):
            got = dot(p, var_ref[:, j * LANES : (j + 1) * LANES])
            at = (kind * 8 + j) * total
            u_ref[at : at + total] = got.reshape(total, 16, LANES)
    acc_ref[...] = jnp.zeros_like(acc_ref)

    def add(q, carry):
        for k in range(8):
            d = bdst_ref[q, k]
            acc_ref[d] = acc_ref[d] + u_ref[bsrc_ref[q, k]]
        return carry

    lax.fori_loop(0, total, add, 0)
    for s in range(slots):
        parts = [acc_ref[s * 4 + k] for k in range(4)]
        r = jnp.where(
            blk < 2 * TS,
            jnp.where(blk < TS, parts[0], parts[1]),
            jnp.where(blk < 3 * TS, parts[2], parts[3]),
        )
        hi = r.astype(jnp.bfloat16)
        r_ref[s, :, :LANES] = hi
        r_ref[s, :, LANES:] = (r - hi.astype(jnp.float32)).astype(jnp.bfloat16)
    add_in = dot(r_ref[...].reshape(slots * 16, 2 * LANES), img_ref[...])
    out = inner_ref[...].reshape(slots * 16, CELLS) + add_in
    out_ref[...] = out.astype(jnp.bfloat16).reshape(slots, 16, CELLS)


def sum_kernel(
    dp_size, tile_size, factor, in_ref, out_ref, src_ref, near_ref, far_ref, all_ref,
    near_send, near_recv, far_send, far_recv, all_send, all_recv,
):
    dp, tile = lax.axis_index("dp"), lax.axis_index("tile")
    pairs = dp_size // 2
    core, hi = lax.rem(dp, 2), dp // 2
    near_count = 2 * tile_size
    chunk = src_ref.shape[1]
    me = core * tile_size + tile
    mesh_ids = pl.DeviceIdType.MESH

    def near_peer(j):
        return (lax.rem(core + j % 2, 2), lax.rem(tile + j // 2, tile_size))

    def near_device(j):
        peer_core, peer_tile = near_peer(j)
        return (hi * 2 + peer_core, peer_tile)

    def far_device(j):
        return (lax.rem(hi + j, pairs) * 2 + core, tile)

    peers = [near_device(j) for j in range(1, near_count)] + [far_device(j) for j in range(1, pairs)]
    barrier = pltpu.get_barrier_semaphore()
    for peer in peers:
        pl.semaphore_signal(barrier, inc=1, device_id=peer, device_id_type=mesh_ids)

    rows = in_ref.shape[0]
    quarter = rows // 4
    rest = in_ref[:, LANES:]
    packed = jnp.concatenate(
        [
            in_ref[:, :LANES],
            jnp.concatenate([rest[k * quarter : (k + 1) * quarter] for k in range(4)], axis=1),
            jnp.zeros((near_count * chunk - rows - quarter, LANES), jnp.float32),
        ],
        axis=0,
    )
    src_ref[...] = packed.reshape(near_count, chunk, LANES)
    near_ref[me] = src_ref[me]
    pl.semaphore_wait(barrier, len(peers))

    def exchange(count, src_of, dst, device_of, send, recv):
        copies = []
        for j in range(1, count):
            copy = pltpu.make_async_remote_copy(
                src_ref=src_of(j),
                dst_ref=dst,
                send_sem=send.at[j],
                recv_sem=recv.at[j],
                device_id=device_of(j),
                device_id_type=mesh_ids,
            )
            copy.start()
            copies.append(copy)
        for copy in copies:
            copy.wait_recv()
        return copies

    def added(ref):
        total = ref[0]
        for j in range(1, ref.shape[0]):
            total = total + ref[j]
        return total

    def chunk_for(j):
        peer_core, peer_tile = near_peer(j)
        return src_ref.at[peer_core * tile_size + peer_tile]

    copies = exchange(near_count, chunk_for, near_ref.at[me], near_device, near_send, near_recv)
    far_ref[hi] = added(near_ref)
    copies += exchange(
        pairs, lambda j: far_ref.at[hi], far_ref.at[hi], far_device, far_send, far_recv
    )
    all_ref[me] = added(far_ref) * factor
    copies += exchange(
        near_count, lambda j: all_ref.at[me], all_ref.at[me], near_device, all_send, all_recv
    )
    whole = all_ref[...].reshape(near_count * chunk, LANES)
    out_ref[:, :LANES] = whole[:rows]
    for k in range(4):
        out_ref[k * quarter : (k + 1) * quarter, LANES:] = whole[
            rows : rows + quarter, k * 32 : (k + 1) * 32
        ]
    for copy in copies:
        copy.wait_send()


def params():
    return pltpu.CompilerParams(vmem_limit_bytes=VMEM_LIMIT)


def cost(flops, bytes_accessed):
    return pl.CostEstimate(flops=flops, bytes_accessed=bytes_accessed, transcendentals=0)


def body(fields, weights, bias, cotangent, neighbours, rotations, tile_map):
    batch_loc, slots, in_chans, cells = fields.shape
    out_chans = weights.shape[0]
    x = fields.reshape(slots, in_chans, cells)
    g = cotangent.reshape(slots, out_chans, cells)
    tiles = 3
    steps = slots // tiles
    f32, bf16 = jnp.float32, jnp.bfloat16
    pick = const(column_picker())
    variants = const(strip_variants())
    vmem = pl.BlockSpec(memory_space=pltpu.VMEM)
    smem = pl.BlockSpec(memory_space=pltpu.SMEM)

    def whole(*dims):
        return pl.BlockSpec(dims, lambda i, *_: (0,) * len(dims))

    def block(*dims):
        return pl.BlockSpec((tiles, *dims), lambda i, *_: (i,) + (0,) * len(dims))

    tile_size, dp_size = lax.axis_size("tile"), lax.axis_size("dp")
    total = tile_size * slots
    wt = weights.transpose(2, 3, 1, 0).reshape(9 * in_chans, out_chans)
    back_tiles = 6
    back_steps = slots // back_tiles
    inner, all_edges, all_rims = pl.pallas_call(
        lambda *refs: gather_kernel(tile_size, *refs),
        grid=(back_steps,),
        out_shape=(
            jax.ShapeDtypeStruct((slots, in_chans, cells), f32),
            jax.ShapeDtypeStruct((total, in_chans, LANES), bf16),
            jax.ShapeDtypeStruct((total, in_chans, 2 * LANES), bf16),
        ),
        in_specs=[
            whole(slots, in_chans, cells),
            pl.BlockSpec((back_tiles, out_chans, cells), lambda i: (i, 0, 0)),
            whole(*wt.shape),
            whole(*pick.shape),
        ],
        out_specs=(
            pl.BlockSpec((back_tiles, in_chans, cells), lambda i: (i, 0, 0)),
            whole(total, in_chans, LANES),
            whole(total, in_chans, 2 * LANES),
        ),
        scratch_shapes=[
            pltpu.VMEM((total, in_chans, LANES), bf16),
            pltpu.VMEM((total, in_chans, 2 * LANES), bf16),
            pltpu.SemaphoreType.DMA((tile_size,)),
            pltpu.SemaphoreType.DMA((tile_size,)),
            pltpu.SemaphoreType.DMA((tile_size, back_steps)),
            pltpu.SemaphoreType.DMA((tile_size, back_steps)),
        ],
        compiler_params=pltpu.CompilerParams(
            collective_id=1, has_side_effects=True, vmem_limit_bytes=VMEM_LIMIT
        ),
        name="back",
    )(x, g, wt, pick)

    fsrc, bsrc, bdst = pl.pallas_call(
        lambda *refs: tables_kernel(slots, *refs),
        out_shape=(jax.ShapeDtypeStruct((total, 8), jnp.int32),) * 3,
        in_specs=[vmem] * 3,
        out_specs=(vmem,) * 3,
        name="tables",
    )(tile_map.reshape(1, total), neighbours, rotations)

    wf = weights.transpose(0, 2, 3, 1).reshape(out_chans, 9 * in_chans)
    images = const(rim_images())
    outputs, sums = pl.pallas_call(
        lambda *refs: front_kernel(slots, *refs),
        grid_spec=pltpu.PrefetchScalarGridSpec(
            num_scalar_prefetch=1,
            grid=(steps,),
            in_specs=[
                whole(*all_edges.shape),
                whole(*variants.shape),
                whole(*images.shape),
                block(in_chans, cells),
                block(out_chans, cells),
                whole(*wf.shape),
                whole(1, out_chans),
            ],
            out_specs=(block(out_chans, cells), whole(out_chans, 160)),
            scratch_shapes=[
                pltpu.VMEM((8 * total, in_chans, LANES), f32),
                pltpu.VMEM((slots, in_chans, 2 * LANES), bf16),
                pltpu.VMEM((slots, in_chans, CELLS + 3 * LANES), f32),
                pltpu.VMEM((tiles, 160, CELLS), bf16),
            ],
        ),
        out_shape=(
            jax.ShapeDtypeStruct((slots, out_chans, cells), bf16),
            jax.ShapeDtypeStruct((out_chans, 160), f32),
        ),
        compiler_params=params(),
        cost_estimate=cost(slots * 1024 * 144 * 256 * 8, slots * 64 * CELLS * 4),
        name="front",
    )(fsrc, all_edges, variants, images, x, g, wf, bias[None, :])
    factor = 1.0 / math.sqrt(
        batch_loc * lax.axis_size("dp") * slots * lax.axis_size("tile") * cells
    )
    near_count, pairs = 2 * tile_size, dp_size // 2
    packed_rows = out_chans + out_chans // 4
    chunk = -(-packed_rows // (8 * near_count)) * 8
    sums = pl.pallas_call(
        lambda *refs: sum_kernel(dp_size, tile_size, factor, *refs),
        out_shape=jax.ShapeDtypeStruct((out_chans, 160), f32),
        in_specs=[vmem],
        out_specs=vmem,
        scratch_shapes=[
            pltpu.VMEM((near_count, chunk, LANES), f32),
            pltpu.VMEM((near_count, chunk, LANES), f32),
            pltpu.VMEM((pairs, chunk, LANES), f32),
            pltpu.VMEM((near_count, chunk, LANES), f32),
            pltpu.SemaphoreType.DMA((near_count,)),
            pltpu.SemaphoreType.DMA((near_count,)),
            pltpu.SemaphoreType.DMA((pairs,)),
            pltpu.SemaphoreType.DMA((pairs,)),
            pltpu.SemaphoreType.DMA((near_count,)),
            pltpu.SemaphoreType.DMA((near_count,)),
        ],
        compiler_params=pltpu.CompilerParams(
            collective_id=0, has_side_effects=True, vmem_limit_bytes=VMEM_LIMIT
        ),
        name="sums",
    )(sums)
    grad_weights = sums[:, :144].reshape(out_chans, 3, 3, in_chans).transpose(0, 3, 1, 2)
    grad_bias = sums[:, 144]

    edge_img = const(edge_images())
    grad_fields = pl.pallas_call(
        lambda *refs: finish_kernel(slots, *refs),
        out_shape=jax.ShapeDtypeStruct((slots, in_chans, cells), bf16),
        in_specs=[smem, smem, vmem, vmem, vmem, vmem],
        out_specs=vmem,
        scratch_shapes=[
            pltpu.VMEM((16 * total, in_chans, LANES), f32),
            pltpu.VMEM((4 * slots + 8, in_chans, LANES), f32),
            pltpu.VMEM((slots, in_chans, 2 * LANES), bf16),
        ],
        compiler_params=params(),
        cost_estimate=cost(slots * 1024 * 144 * 128 * 8, slots * 64 * CELLS * 4),
        name="finish",
    )(bsrc, bdst, all_rims, variants, edge_img, inner)
    return (
        outputs.reshape(cotangent.shape),
        grad_fields.reshape(fields.shape),
        grad_weights,
        grad_bias,
    )


def solution(mesh):
    placed = (P("dp", "tile", None, None), P(), P(), P("dp", "tile", None, None), P(), P(), P())
    return jax.shard_map(
        body,
        mesh=mesh,
        in_specs=placed,
        out_specs=(P("dp", "tile", None, None), P("dp", "tile", None, None), P(), P()),
        check_vma=False,
    )
```

```python
import math

import jax
import jax.numpy as jnp
import numpy as np
from jax import lax
from jax.experimental import pallas as pl
from jax.experimental.pallas import tpu as pltpu
from jax.sharding import PartitionSpec as P

TS = 32


edge_table = np.array(
    [
        [1, 2, 0, 3],
        [0, 3, 1, 2],
        [3, 1, 2, 0],
        [2, 0, 3, 1],
        [1, 1, 0, 0],
        [1, 0, 0, 1],
        [0, 1, 1, 0],
        [0, 0, 1, 1],
    ],
    dtype=np.int32,
)
flip_table = np.array(
    [
        [0, 0, 1, 1],
        [0, 0, 1, 1],
        [0, 1, 1, 0],
        [0, 1, 1, 0],
        [1, 0, 0, 1],
        [0, 0, 1, 1],
        [1, 1, 0, 0],
        [0, 1, 1, 0],
    ],
    dtype=np.int32,
)


def tables_kernel(slots, map_ref, nbr_ref, rot_ref, fsrc_ref, bsrc_ref, bdst_ref):
    total = map_ref.shape[1]
    base = lax.axis_index("tile") * slots
    held = map_ref[...].astype(jnp.float32)
    rows = lax.broadcasted_iota(jnp.int32, (total, total), 0)
    cols = lax.broadcasted_iota(jnp.int32, (total, total), 1)
    places = cols.astype(jnp.float32)
    held_col = jnp.sum(jnp.where(rows == cols, held, 0.0), axis=1, keepdims=True)
    onehot = jnp.where(held_col == places, 1.0, 0.0).astype(jnp.bfloat16)
    tile_nbr = dot_last(onehot, nbr_ref[...].astype(jnp.float32).astype(jnp.bfloat16))
    tile_rot = dot_last(onehot, rot_ref[...].astype(jnp.float32).astype(jnp.bfloat16))
    k_ids = lax.broadcasted_iota(jnp.int32, (total, 8), 1)
    s_ids = lax.broadcasted_iota(jnp.int32, (total, 8), 0)
    nbr = jnp.zeros((total, 8), jnp.float32)
    edge = jnp.zeros((total, 8), jnp.int32)
    flip = jnp.zeros((total, 8), jnp.int32)
    for k in range(8):
        found = jnp.where(held == tile_nbr[:, k : k + 1], places, 0.0)
        nbr = jnp.where(k_ids == k, jnp.sum(found, axis=1, keepdims=True), nbr)
        for r in range(4):
            here = (k_ids == k) & (tile_rot == float(r))
            edge = jnp.where(here, int(edge_table[k, r]), edge)
            flip = jnp.where(here, int(flip_table[k, r]), flip)
    nbr = nbr.astype(jnp.int32)
    fsrc_ref[...] = (edge * 2 + flip) * total + nbr
    bsrc_ref[...] = (k_ids * 2 + flip) * total + s_ids
    own = nbr - base
    bdst_ref[...] = jnp.where((own >= 0) & (own < slots), own * 4 + edge, slots * 4)


CELLS = TS * TS
LANES = 128
VMEM_LIMIT = 50 * 1024 * 1024


def column_picker():
    m = np.zeros((CELLS, LANES), np.float32)
    for h in range(TS):
        m[h * TS, 2 * TS + h] = 1
        m[h * TS + TS - 1, 3 * TS + h] = 1
    return m


def strip_variants():
    m = np.zeros((LANES, 8 * LANES), np.float32)
    for edge in range(4):
        for flip in range(2):
            for rep in range(4):
                for t in range(TS):
                    at = TS - 1 - t if flip else t
                    m[edge * TS + at, (edge * 2 + flip) * LANES + rep * TS + t] = 1
    return m


def rim_images():
    m = np.zeros((2 * LANES, CELLS + 3 * LANES), np.float32)
    for h in range(TS):
        m[2 * TS + h, h * TS] = 1
        m[3 * TS + h, h * TS + TS - 1] = 1
    tops = [LANES] + list(range(TS)) + [LANES + TS]
    lows = [LANES + 2 * TS] + list(range(TS, 2 * TS)) + [LANES + 3 * TS]
    for col_tap in range(3):
        for w in range(TS):
            m[tops[w + col_tap], CELLS + col_tap * LANES + w] = 1
            m[lows[w + col_tap], CELLS + col_tap * LANES + 3 * TS + w] = 1
    return m


def edge_images():
    m = np.zeros((LANES, CELLS), np.float32)
    for t in range(TS):
        m[t, t] = 1
        m[TS + t, (TS - 1) * TS + t] = 1
        m[2 * TS + t, t * TS] = 1
        m[3 * TS + t, t * TS + TS - 1] = 1
    return np.concatenate([m, m], axis=0)


def const(m):
    return jnp.asarray(m.astype(jnp.bfloat16))


def dot(a, b):
    return jnp.dot(a, b, preferred_element_type=jnp.float32)


def dot_last(a, b):
    return lax.dot_general(a, b, (((1,), (1,)), ((), ())), preferred_element_type=jnp.float32)


def lane_ids(width):
    return lax.broadcasted_iota(jnp.int32, (16, width), 1)


def gather_kernel(
    tile_size, x_ref, g_ref, wt_ref, pick_ref, inner_ref, edges_ref, rims_ref,
    q_all, p_all, q_send, q_recv, p_send, p_recv,
):
    step = pl.program_id(0)
    slots, tiles = x_ref.shape[0], g_ref.shape[0]
    steps = slots // tiles
    dp, tile = lax.axis_index("dp"), lax.axis_index("tile")
    base = tile * slots
    barrier = pltpu.get_barrier_semaphore()
    mesh_ids = pl.DeviceIdType.MESH

    def peer(j):
        return (dp, lax.rem(tile + j, tile_size))

    def edges_copy(j):
        part = q_all.at[pl.ds(base, slots)]
        return pltpu.make_async_remote_copy(
            src_ref=part, dst_ref=part, send_sem=q_send.at[j], recv_sem=q_recv.at[j],
            device_id=peer(j), device_id_type=mesh_ids,
        )

    def rims_copy(j, i):
        part = p_all.at[pl.ds(base + i * tiles, tiles)]
        return pltpu.make_async_remote_copy(
            src_ref=part, dst_ref=part, send_sem=p_send.at[j, i], recv_sem=p_recv.at[j, i],
            device_id=peer(j), device_id_type=mesh_ids,
        )

    @pl.when(step == 0)
    def _():
        for j in range(1, tile_size):
            pl.semaphore_signal(barrier, inc=1, device_id=peer(j), device_id_type=mesh_ids)
        x = x_ref[...].reshape(slots * 16, CELLS)
        cols = dot(x, pick_ref[...])
        first = x[:, :LANES].astype(jnp.float32)
        last = pltpu.roll(x[:, CELLS - LANES :].astype(jnp.float32), 2 * TS, 1)
        lane = lax.broadcasted_iota(jnp.int32, (slots * 16, LANES), 1)
        q = jnp.where(lane < TS, first, jnp.where(lane < 2 * TS, last, cols))
        q_all[pl.ds(base, slots)] = q.astype(jnp.bfloat16).reshape(slots, 16, LANES)

    lane = lane_ids(CELLS)
    w = lane % TS
    blk = lane_ids(LANES)

    def rows_added(y):
        up = jnp.where(lane < CELLS - TS, pltpu.roll(y[0], CELLS - TS, 1), 0.0)
        down = jnp.where(lane >= TS, pltpu.roll(y[2], TS, 1), 0.0)
        return y[1] + up + down

    kept, sides = [], []
    for t in range(tiles):
        z = dot(wt_ref[...], g_ref[t])
        rows, rim = [], []
        for a in range(3):
            z0, z1, z2 = (z[(a * 3 + c) * 16 : (a * 3 + c + 1) * 16] for c in range(3))
            rows.append(
                z1
                + jnp.where(w != TS - 1, pltpu.roll(z0, CELLS - 1, 1), 0.0)
                + jnp.where(w != 0, pltpu.roll(z2, 1, 1), 0.0)
            )
            rim.append(jnp.where(w == 0, z0, jnp.where(w == TS - 1, z2, 0.0)))
        inner_ref[t] = rows_added(rows)
        sides.append(rows_added(rim).astype(jnp.bfloat16))
        c0 = rim[0][:, :LANES]
        c2 = rim[2][:, CELLS - LANES :]
        corner = jnp.where(blk == 0, c0, 0.0)
        corner += jnp.where(blk == TS, pltpu.roll(c0, 1, 1), 0.0)
        corner += jnp.where(blk == 2 * TS, pltpu.roll(c2, LANES - TS, 1), 0.0)
        corner += jnp.where(blk == 3 * TS, pltpu.roll(c2, LANES - TS + 1, 1), 0.0)
        kept.append((rows[0][:, :LANES], rows[2][:, CELLS - LANES :], corner))
    cols = dot(jnp.concatenate(sides, axis=0), pick_ref[...])
    for t in range(tiles):
        first, last, corner = kept[t]
        edge = jnp.where(
            blk < TS,
            first,
            jnp.where(blk < 2 * TS, pltpu.roll(last, 2 * TS, 1), cols[t * 16 : (t + 1) * 16]),
        )
        both = jnp.concatenate([edge, corner], axis=1)
        p_all[base + step * tiles + t] = both.astype(jnp.bfloat16)

    @pl.when(step == 0)
    def _():
        pl.semaphore_wait(barrier, tile_size - 1)
        for j in range(1, tile_size):
            edges_copy(j).start()

    for j in range(1, tile_size):
        rims_copy(j, step).start()

    @pl.when(step == steps - 1)
    def _():
        for j in range(1, tile_size):
            edges_copy(j).wait()
            for i in range(steps):
                rims_copy(j, i).wait()
        edges_ref[...] = q_all[...]
        rims_ref[...] = p_all[...]


def front_kernel(
    slots, fsrc_ref, q_ref, var_ref, img_ref, x_ref, g_ref, w_ref, bias_ref,
    out_ref, dw_ref, v_ref, rim_ref, ri_ref, col_ref,
):
    step = pl.program_id(0)
    blk = lane_ids(LANES)

    @pl.when(step == 0)
    def _():
        total = q_ref.shape[0]
        base = lax.axis_index("tile") * slots
        q = q_ref[...].reshape(total * 16, LANES)
        for j in range(8):
            got = dot(q, var_ref[:, j * LANES : (j + 1) * LANES])
            v_ref[j * total : (j + 1) * total] = got.reshape(total, 16, LANES)
        for s in range(slots):
            for half in range(2):
                parts = [v_ref[fsrc_ref[base + s, half * 4 + k]] for k in range(4)]
                rim = jnp.where(
                    blk < 2 * TS,
                    jnp.where(blk < TS, parts[0], parts[1]),
                    jnp.where(blk < 3 * TS, parts[2], parts[3]),
                )
                rim_ref[s, :, half * LANES : (half + 1) * LANES] = rim.astype(jnp.bfloat16)
        ri = dot(rim_ref[...].reshape(slots * 16, 2 * LANES), img_ref[...])
        ri_ref[...] = ri.reshape(slots, 16, CELLS + 3 * LANES)
        dw_ref[...] = jnp.zeros_like(dw_ref)
        for t in range(col_ref.shape[0]):
            col_ref[t, 144:160, :] = jnp.ones((16, CELLS), jnp.bfloat16)

    w = lane_ids(CELLS) % TS
    tiles = x_ref.shape[0]
    chans = bias_ref.shape[1]
    same = lax.broadcasted_iota(jnp.int32, (chans, chans), 0) == lax.broadcasted_iota(
        jnp.int32, (chans, chans), 1
    )
    bias = jnp.sum(jnp.where(same, bias_ref[...], 0.0), axis=1, keepdims=True)
    total = jnp.zeros(dw_ref.shape, jnp.float32)
    for t in range(tiles):
        s = step * tiles + t
        x = x_ref[t].astype(jnp.float32)
        lr = ri_ref[s, :, :CELLS]
        mids = [
            jnp.where(w == 0, lr, pltpu.roll(x, 1, 1)),
            x,
            jnp.where(w == TS - 1, lr, pltpu.roll(x, CELLS - 1, 1)),
        ]
        for c in range(3):
            rim = ri_ref[s, :, CELLS + c * LANES : CELLS + (c + 1) * LANES]
            down = pltpu.roll(mids[c], TS, 1)
            up = pltpu.roll(mids[c], CELLS - TS, 1)
            down = jnp.concatenate(
                [jnp.where(blk < TS, rim, down[:, :LANES]), down[:, LANES:]], axis=1
            )
            up = jnp.concatenate(
                [up[:, : CELLS - LANES], jnp.where(blk >= 3 * TS, rim, up[:, CELLS - LANES :])],
                axis=1,
            )
            for a, tap in enumerate((down, mids[c], up)):
                row = (a * 3 + c) * 16
                col_ref[t, row : row + 16, :] = tap.astype(jnp.bfloat16)
        col = col_ref[t]
        out_ref[t] = (dot(w_ref[...], col[:144]) + bias).astype(jnp.bfloat16)
        total += lax.dot_general(
            g_ref[t], col, (((1,), (1,)), ((), ())), preferred_element_type=jnp.float32
        )
    dw_ref[...] += total


def finish_kernel(slots, bsrc_ref, bdst_ref, p_ref, var_ref, img_ref, inner_ref, out_ref, u_ref, acc_ref, r_ref):
    total = p_ref.shape[0]
    blk = lane_ids(LANES)
    for kind in range(2):
        p = p_ref[:, :, kind * LANES : (kind + 1) * LANES].reshape(total * 16, LANES)
        for j in range(8):
            got = dot(p, var_ref[:, j * LANES : (j + 1) * LANES])
            at = (kind * 8 + j) * total
            u_ref[at : at + total] = got.reshape(total, 16, LANES)
    acc_ref[...] = jnp.zeros_like(acc_ref)

    def add(q, carry):
        for k in range(8):
            d = bdst_ref[q, k]
            acc_ref[d] = acc_ref[d] + u_ref[bsrc_ref[q, k]]
        return carry

    lax.fori_loop(0, total, add, 0)
    for s in range(slots):
        parts = [acc_ref[s * 4 + k] for k in range(4)]
        r = jnp.where(
            blk < 2 * TS,
            jnp.where(blk < TS, parts[0], parts[1]),
            jnp.where(blk < 3 * TS, parts[2], parts[3]),
        )
        hi = r.astype(jnp.bfloat16)
        r_ref[s, :, :LANES] = hi
        r_ref[s, :, LANES:] = (r - hi.astype(jnp.float32)).astype(jnp.bfloat16)
    add_in = dot(r_ref[...].reshape(slots * 16, 2 * LANES), img_ref[...])
    out = inner_ref[...].reshape(slots * 16, CELLS) + add_in
    out_ref[...] = out.astype(jnp.bfloat16).reshape(slots, 16, CELLS)


def sum_kernel(
    dp_size, tile_size, factor, in_ref, out_ref, src_ref, near_ref, far_ref, all_ref,
    near_send, near_recv, far_send, far_recv, all_send, all_recv,
):
    dp, tile = lax.axis_index("dp"), lax.axis_index("tile")
    pairs = dp_size // 2
    core, hi = lax.rem(dp, 2), dp // 2
    near_count = 2 * tile_size
    chunk = src_ref.shape[1]
    me = core * tile_size + tile
    mesh_ids = pl.DeviceIdType.MESH

    def near_peer(j):
        return (lax.rem(core + j % 2, 2), lax.rem(tile + j // 2, tile_size))

    def near_device(j):
        peer_core, peer_tile = near_peer(j)
        return (hi * 2 + peer_core, peer_tile)

    def far_device(j):
        return (lax.rem(hi + j, pairs) * 2 + core, tile)

    peers = [near_device(j) for j in range(1, near_count)] + [far_device(j) for j in range(1, pairs)]
    barrier = pltpu.get_barrier_semaphore()
    for peer in peers:
        pl.semaphore_signal(barrier, inc=1, device_id=peer, device_id_type=mesh_ids)

    rows = in_ref.shape[0]
    quarter = rows // 4
    rest = in_ref[:, LANES:]
    packed = jnp.concatenate(
        [
            in_ref[:, :LANES],
            jnp.concatenate([rest[k * quarter : (k + 1) * quarter] for k in range(4)], axis=1),
            jnp.zeros((near_count * chunk - rows - quarter, LANES), jnp.float32),
        ],
        axis=0,
    )
    src_ref[...] = packed.reshape(near_count, chunk, LANES)
    near_ref[me] = src_ref[me]
    pl.semaphore_wait(barrier, len(peers))

    def exchange(count, src_of, dst, device_of, send, recv):
        copies = []
        for j in range(1, count):
            copy = pltpu.make_async_remote_copy(
                src_ref=src_of(j),
                dst_ref=dst,
                send_sem=send.at[j],
                recv_sem=recv.at[j],
                device_id=device_of(j),
                device_id_type=mesh_ids,
            )
            copy.start()
            copies.append(copy)
        for copy in copies:
            copy.wait_recv()
        return copies

    def added(ref):
        total = ref[0]
        for j in range(1, ref.shape[0]):
            total = total + ref[j]
        return total

    def chunk_for(j):
        peer_core, peer_tile = near_peer(j)
        return src_ref.at[peer_core * tile_size + peer_tile]

    copies = exchange(near_count, chunk_for, near_ref.at[me], near_device, near_send, near_recv)
    far_ref[hi] = added(near_ref)
    copies += exchange(
        pairs, lambda j: far_ref.at[hi], far_ref.at[hi], far_device, far_send, far_recv
    )
    all_ref[me] = added(far_ref) * factor
    copies += exchange(
        near_count, lambda j: all_ref.at[me], all_ref.at[me], near_device, all_send, all_recv
    )
    whole = all_ref[...].reshape(near_count * chunk, LANES)
    out_ref[:, :LANES] = whole[:rows]
    for k in range(4):
        out_ref[k * quarter : (k + 1) * quarter, LANES:] = whole[
            rows : rows + quarter, k * 32 : (k + 1) * 32
        ]
    for copy in copies:
        copy.wait_send()


def params():
    return pltpu.CompilerParams(vmem_limit_bytes=VMEM_LIMIT)


def cost(flops, bytes_accessed):
    return pl.CostEstimate(flops=flops, bytes_accessed=bytes_accessed, transcendentals=0)


def body(fields, weights, bias, cotangent, neighbours, rotations, tile_map):
    batch_loc, slots, in_chans, cells = fields.shape
    out_chans = weights.shape[0]
    x = fields.reshape(slots, in_chans, cells)
    g = cotangent.reshape(slots, out_chans, cells)
    tiles = 3
    steps = slots // tiles
    f32, bf16 = jnp.float32, jnp.bfloat16
    pick = const(column_picker())
    variants = const(strip_variants())
    vmem = pl.BlockSpec(memory_space=pltpu.VMEM)
    smem = pl.BlockSpec(memory_space=pltpu.SMEM)

    def whole(*dims):
        return pl.BlockSpec(dims, lambda i, *_: (0,) * len(dims))

    def block(*dims):
        return pl.BlockSpec((tiles, *dims), lambda i, *_: (i,) + (0,) * len(dims))

    tile_size, dp_size = lax.axis_size("tile"), lax.axis_size("dp")
    total = tile_size * slots
    wt = weights.transpose(2, 3, 1, 0).reshape(9 * in_chans, out_chans)
    back_tiles = 6
    back_steps = slots // back_tiles
    inner, all_edges, all_rims = pl.pallas_call(
        lambda *refs: gather_kernel(tile_size, *refs),
        grid=(back_steps,),
        out_shape=(
            jax.ShapeDtypeStruct((slots, in_chans, cells), f32),
            jax.ShapeDtypeStruct((total, in_chans, LANES), bf16),
            jax.ShapeDtypeStruct((total, in_chans, 2 * LANES), bf16),
        ),
        in_specs=[
            whole(slots, in_chans, cells),
            pl.BlockSpec((back_tiles, out_chans, cells), lambda i: (i, 0, 0)),
            whole(*wt.shape),
            whole(*pick.shape),
        ],
        out_specs=(
            pl.BlockSpec((back_tiles, in_chans, cells), lambda i: (i, 0, 0)),
            whole(total, in_chans, LANES),
            whole(total, in_chans, 2 * LANES),
        ),
        scratch_shapes=[
            pltpu.VMEM((total, in_chans, LANES), bf16),
            pltpu.VMEM((total, in_chans, 2 * LANES), bf16),
            pltpu.SemaphoreType.DMA((tile_size,)),
            pltpu.SemaphoreType.DMA((tile_size,)),
            pltpu.SemaphoreType.DMA((tile_size, back_steps)),
            pltpu.SemaphoreType.DMA((tile_size, back_steps)),
        ],
        compiler_params=pltpu.CompilerParams(
            collective_id=1, has_side_effects=True, vmem_limit_bytes=VMEM_LIMIT
        ),
        name="back",
    )(x, g, wt, pick)

    fsrc, bsrc, bdst = pl.pallas_call(
        lambda *refs: tables_kernel(slots, *refs),
        out_shape=(jax.ShapeDtypeStruct((total, 8), jnp.int32),) * 3,
        in_specs=[vmem] * 3,
        out_specs=(vmem,) * 3,
        name="tables",
    )(tile_map.reshape(1, total), neighbours.T, rotations.T)

    wf = weights.transpose(0, 2, 3, 1).reshape(out_chans, 9 * in_chans)
    images = const(rim_images())
    outputs, sums = pl.pallas_call(
        lambda *refs: front_kernel(slots, *refs),
        grid_spec=pltpu.PrefetchScalarGridSpec(
            num_scalar_prefetch=1,
            grid=(steps,),
            in_specs=[
                whole(*all_edges.shape),
                whole(*variants.shape),
                whole(*images.shape),
                block(in_chans, cells),
                block(out_chans, cells),
                whole(*wf.shape),
                whole(1, out_chans),
            ],
            out_specs=(block(out_chans, cells), whole(out_chans, 160)),
            scratch_shapes=[
                pltpu.VMEM((8 * total, in_chans, LANES), f32),
                pltpu.VMEM((slots, in_chans, 2 * LANES), bf16),
                pltpu.VMEM((slots, in_chans, CELLS + 3 * LANES), f32),
                pltpu.VMEM((tiles, 160, CELLS), bf16),
            ],
        ),
        out_shape=(
            jax.ShapeDtypeStruct((slots, out_chans, cells), bf16),
            jax.ShapeDtypeStruct((out_chans, 160), f32),
        ),
        compiler_params=params(),
        cost_estimate=cost(slots * 1024 * 144 * 256 * 8, slots * 64 * CELLS * 4),
        name="front",
    )(fsrc, all_edges, variants, images, x, g, wf, bias[None, :])
    factor = 1.0 / math.sqrt(
        batch_loc * lax.axis_size("dp") * slots * lax.axis_size("tile") * cells
    )
    near_count, pairs = 2 * tile_size, dp_size // 2
    packed_rows = out_chans + out_chans // 4
    chunk = -(-packed_rows // (8 * near_count)) * 8
    sums = pl.pallas_call(
        lambda *refs: sum_kernel(dp_size, tile_size, factor, *refs),
        out_shape=jax.ShapeDtypeStruct((out_chans, 160), f32),
        in_specs=[vmem],
        out_specs=vmem,
        scratch_shapes=[
            pltpu.VMEM((near_count, chunk, LANES), f32),
            pltpu.VMEM((near_count, chunk, LANES), f32),
            pltpu.VMEM((pairs, chunk, LANES), f32),
            pltpu.VMEM((near_count, chunk, LANES), f32),
            pltpu.SemaphoreType.DMA((near_count,)),
            pltpu.SemaphoreType.DMA((near_count,)),
            pltpu.SemaphoreType.DMA((pairs,)),
            pltpu.SemaphoreType.DMA((pairs,)),
            pltpu.SemaphoreType.DMA((near_count,)),
            pltpu.SemaphoreType.DMA((near_count,)),
        ],
        compiler_params=pltpu.CompilerParams(
            collective_id=0, has_side_effects=True, vmem_limit_bytes=VMEM_LIMIT
        ),
        name="sums",
    )(sums)
    grad_weights = sums[:, :144].reshape(out_chans, 3, 3, in_chans).transpose(0, 3, 1, 2)
    grad_bias = sums[:, 144]

    edge_img = const(edge_images())
    grad_fields = pl.pallas_call(
        lambda *refs: finish_kernel(slots, *refs),
        out_shape=jax.ShapeDtypeStruct((slots, in_chans, cells), bf16),
        in_specs=[smem, smem, vmem, vmem, vmem, vmem],
        out_specs=vmem,
        scratch_shapes=[
            pltpu.VMEM((16 * total, in_chans, LANES), f32),
            pltpu.VMEM((4 * slots + 8, in_chans, LANES), f32),
            pltpu.VMEM((slots, in_chans, 2 * LANES), bf16),
        ],
        compiler_params=params(),
        cost_estimate=cost(slots * 1024 * 144 * 128 * 8, slots * 64 * CELLS * 4),
        name="finish",
    )(bsrc, bdst, all_rims, variants, edge_img, inner)
    return (
        outputs.reshape(cotangent.shape),
        grad_fields.reshape(fields.shape),
        grad_weights,
        grad_bias,
    )


def solution(mesh):
    placed = (P("dp", "tile", None, None), P(), P(), P("dp", "tile", None, None), P(), P(), P())
    return jax.shard_map(
        body,
        mesh=mesh,
        in_specs=placed,
        out_specs=(P("dp", "tile", None, None), P("dp", "tile", None, None), P(), P()),
        check_vma=False,
    )
```
